128 devices in a mesh: feat: 8 (over y, core), node: 16 (over x, z).
Axes of the slice: x: 4, y: 4, z: 4, core: 2. Of those that a mesh axis runs over, the one named last changes fastest.
Arguments:
- features: bfloat16 [128, 98304], P('feat', 'node'), may hold values from -6 to 6
- tile_cols: int32 [768, 16], P('node'), may hold values from 0 to 767, as said below
- tile_counts: int32 [768], P('node'), may hold values from 1 to 16, as said below
- tiles: bfloat16 [768, 16, 128, 128], P('node'), may hold values from 0 to 2, as said below
- degrees: int32 [98304], P('node'), may hold values from 8 to 32
- weights1: bfloat16 [2, 128, 256], P(None, 'feat'), may hold values from -0.5 to 0.5
- bias1: float32 [256], replicated, may hold values from -3 to 3
- weights2: bfloat16 [2, 256, 256], P(None, 'feat'), may hold values from -0.375 to 0.375
- bias2: float32 [256], replicated, may hold values from -3 to 3
- cotangent: bfloat16 [98304, 256], P(('node', 'feat')), may hold values from -6 to 6
Outputs:
- hidden_out: bfloat16 [98304, 256], P(('node', 'feat'))
- grad_second: float32 [2, 256, 256], P(None, 'feat')
- grad_first: float32 [2, 128, 256], P(None, 'feat')
The draws below stay inside these ranges and needn't reach their ends.
Inputs may be any that keep to these rules, and one draw needn't show every extreme that they name: `tile_cols`: the first tile_counts[r] column blocks of a row block are distinct; later slots are unused. `tile_counts`: 16 is reached in every draw; node shards differ in their load. `tiles`: each entry is zero or a positive edge weight.
All inputs are finite; a program needn't handle non-finite values.
Results may differ from the reference program's by a relative error of at most 0.0055.
Values may be sent and summed in bfloat16 or wider, within the bound.
A program may use at most 128 MiB of HBM per device.

```python
import math
import jax
import jax.numpy as jnp
from jax import lax

F = 128
H = 256
BLK = 128
MAXT = 16
NB_DEV = 48
NB = 768
NODES = 98304


def draw_tile_cols(key, part):
    key = jax.random.fold_in(key, 12)
    row_keys = jax.random.split(key, NB)
    shuffled = jax.vmap(lambda single: jax.random.permutation(single, NB))(row_keys)
    return shuffled[:, :MAXT].astype(jnp.int32)


def draw_tile_counts(key, part):
    key = jax.random.fold_in(key, 11)
    key_heavy, key_forced, key_counts = jax.random.split(key, 3)
    shard_total = NB // NB_DEV
    heavy_shard = jax.random.randint(key_heavy, (shard_total,), 0, 4) == 0
    forced_block = jax.random.randint(key_forced, (), 0, NB)
    shard_index = jnp.arange(shard_total, dtype=jnp.int32)
    heavy_shard = heavy_shard | (shard_index == forced_block // NB_DEV)
    shard_cap = jnp.where(heavy_shard, MAXT, MAXT // 4)
    block_cap = jnp.repeat(shard_cap, NB_DEV)
    raw_counts = jax.random.randint(key_counts, (NB,), 0, 1 << 20)
    counts = raw_counts % block_cap + 1
    block_index = jnp.arange(NB, dtype=jnp.int32)
    return jnp.where(block_index == forced_block, MAXT, counts).astype(jnp.int32)


def draw_tiles(key, part):
    key = jax.random.fold_in(key, 13)
    key_mask, key_weight = jax.random.split(key)
    tile_shape = (NB, MAXT, BLK, BLK)
    present = jax.random.uniform(key_mask, tile_shape, jnp.float32) < 0.125
    edge_weight = jax.random.uniform(key_weight, tile_shape, jnp.float32, 0.5, 1.5)
    return jnp.where(present, edge_weight, 0.0).astype(jnp.bfloat16)


def place_ends(array, key, smallest, high):
    extent = array.shape
    index_at = [jax.random.randint(jax.random.fold_in(key, axis), (), 0, extent[axis]) for axis in range(len(extent))]
    array = array.at[tuple(index_at)].set(smallest)
    longest = extent.index(max(extent))
    index_at[longest] = (index_at[longest] + 1) % extent[longest]
    return array.at[tuple(index_at)].set(high)


def block_levels(stream_key, dims, cuts, low, largest):
    loudness = 1.0
    for axis_at, parts in cuts:
        steps = jax.random.uniform(jax.random.fold_in(jax.random.fold_in(stream_key, 6), axis_at), (parts,), jnp.float32, low / len(cuts), largest / len(cuts))
        loudness = loudness * jnp.repeat(jnp.exp(steps), dims[axis_at] // parts).reshape((-1,) + (1,) * (len(dims) - 1 - axis_at))
    return loudness


def normal_values(key, extent, width, reach, cuts=(), kind=jnp.bfloat16):
    values = width * jax.random.normal(key, extent, jnp.float32)
    if cuts:
        values = values * block_levels(key, extent, cuts, -0.22, 0.18)
    return jnp.clip(values, -reach, reach).astype(kind)


def setup_inputs(seed: int = 0) -> dict:
    seeds = jax.random.split(jax.random.key(seed), 11)
    features = normal_values(seeds[0], (F, NODES), 1.0, 6.0, ((0, 8), (1, 16)))
    tile_cols = draw_tile_cols(jax.random.fold_in(seeds[10], 71), 0)
    tile_counts = draw_tile_counts(jax.random.fold_in(seeds[10], 71), 0)
    tiles = draw_tiles(jax.random.fold_in(seeds[10], 71), 0)
    degrees = place_ends(jax.random.randint(seeds[4], (NODES,), max(1, BLK // 16), BLK // 4 + 1), jax.random.fold_in(seeds[4], 1), max(1, BLK // 16), (BLK // 4 + 1) - 1).astype(jnp.int32)
    weights1 = normal_values(seeds[5], (2, F, H), F ** -0.5, 0.5, ((1, 8),))
    bias1 = normal_values(seeds[6], (H,), 0.5, 3.0, (), jnp.float32)
    weights2 = normal_values(seeds[7], (2, H, H), H ** -0.5, 0.375, ((1, 8),))
    bias2 = normal_values(seeds[8], (H,), 0.5, 3.0, (), jnp.float32)
    cotangent = normal_values(seeds[9], (NODES, H), 1.0, 6.0, ((0, 128),))
    return dict(features=features, tile_cols=tile_cols, tile_counts=tile_counts, tiles=tiles, degrees=degrees, weights1=weights1, bias1=bias1, weights2=weights2, bias2=bias2, cotangent=cotangent)


def aggregate(values, tile_cols, tile_counts, tiles):
    tile_edge = tiles.shape[-1]
    blocks = values.reshape(tiles.shape[0], tile_edge, values.shape[1])
    alive_mask = jnp.arange(tiles.shape[1], dtype=jnp.int32)[None, :] < tile_counts[:, None]

    def per_block(inputs):
        block_cols, alive_row, tile_row = inputs
        source = blocks[block_cols].astype(jnp.float32) * alive_row[:, None, None].astype(jnp.float32)
        return jnp.einsum('tds,tsw->dw', tile_row.astype(jnp.float32), source, precision=lax.Precision.HIGHEST)
    result = lax.map(per_block, (tile_cols, alive_mask, tiles))
    return result.reshape(values.shape[0], values.shape[1])

def aggregate_back(values, tile_cols, tile_counts, tiles):
    tile_edge = tiles.shape[-1]
    blocks = values.reshape(tiles.shape[0], tile_edge, values.shape[1])
    alive_mask = jnp.arange(tiles.shape[1], dtype=jnp.int32)[None, :] < tile_counts[:, None]

    def scan_step(totals, inputs):
        block_cols, alive_row, tile_row, block_vals = inputs
        contrib = jnp.einsum('tds,dw->tsw', tile_row.astype(jnp.float32), block_vals.astype(jnp.float32), precision=lax.Precision.HIGHEST)
        contrib = contrib * alive_row[:, None, None].astype(jnp.float32)
        return (totals.at[block_cols].add(contrib), None)
    start_totals = jnp.zeros(blocks.shape, jnp.float32)
    totals, unused = lax.scan(scan_step, start_totals, (tile_cols, alive_mask, tiles, blocks))
    return totals.reshape(values.shape[0], values.shape[1])

def reference(features, tile_cols, tile_counts, tiles, degrees, weights1, bias1, weights2, bias2, cotangent):
    degree_col = degrees.astype(jnp.float32)[:, None]
    node_feats = features.T
    feat_mean = (aggregate(node_feats, tile_cols, tile_counts, tiles) / degree_col).astype(jnp.bfloat16)
    pre_first = jnp.dot(node_feats, weights1[0], preferred_element_type=jnp.float32) + jnp.dot(feat_mean, weights1[1], preferred_element_type=jnp.float32) + bias1
    sigmoid_pre = jax.nn.sigmoid(pre_first)
    hidden = (pre_first * sigmoid_pre).astype(jnp.bfloat16)
    slope = (sigmoid_pre * (1.0 + pre_first * (1.0 - sigmoid_pre))).astype(jnp.bfloat16)
    hidden_mean = (aggregate(hidden, tile_cols, tile_counts, tiles) / degree_col).astype(jnp.bfloat16)
    hidden_out = (jnp.dot(hidden, weights2[0], preferred_element_type=jnp.float32) + jnp.dot(hidden_mean, weights2[1], preferred_element_type=jnp.float32) + bias2).astype(jnp.bfloat16)
    scale_factor = 1.0 / math.sqrt(features.shape[1])
    grad_second = jnp.stack([jnp.dot(hidden.T, cotangent, preferred_element_type=jnp.float32), jnp.dot(hidden_mean.T, cotangent, preferred_element_type=jnp.float32)]) * scale_factor
    self_grad = jnp.dot(cotangent, weights2[0].T, preferred_element_type=jnp.float32)
    spread = (jnp.dot(cotangent, weights2[1].T, preferred_element_type=jnp.float32) / degree_col).astype(jnp.bfloat16)
    back_mean = aggregate_back(spread, tile_cols, tile_counts, tiles)
    grad_pre = ((self_grad + back_mean) * slope.astype(jnp.float32)).astype(jnp.bfloat16)
    grad_first = jnp.stack([jnp.dot(features, grad_pre, preferred_element_type=jnp.float32), jnp.dot(feat_mean.T, grad_pre, preferred_element_type=jnp.float32)]) * scale_factor
    return (hidden_out, grad_second, grad_first)
```

```python
import functools
import math

import jax
import jax.numpy as jnp
from jax import lax
from jax.experimental import pallas as pl
from jax.experimental.pallas import tpu as pltpu
from jax.sharding import PartitionSpec as P

MESH = pl.DeviceIdType.MESH
BF16 = jnp.bfloat16
F32 = jnp.float32
FEATS = 8
SIDE = 4
BLK = 128
NB = 48
OWN = NB // FEATS
HALF, QUARTER = NB // 2, NB // 4
GROUP = 4
BATCH = 4
STAGES = 4
AHEAD = (0, -1, 1, 2)
VMEM = pl.BlockSpec(memory_space=pltpu.VMEM)
SMEM = pl.BlockSpec(memory_space=pltpu.SMEM)
ANY = pl.BlockSpec(memory_space=pl.ANY)


def dot(left, right, dims):
    return lax.dot_general(left, right, (dims, ((), ())), preferred_element_type=F32)


class Place:
    def __init__(self):
        self.feat = lax.axis_index("feat")
        self.node = lax.axis_index("node")
        self.x = self.node // SIDE
        self.z = self.node % SIDE

    def peer(self, step):
        return (self.feat + step) % FEATS

    def shift(self, dx, dz):
        return ((self.x + dx + SIDE) % SIDE) * SIDE + (self.z + dz + SIDE) % SIDE

    def turned(self, half, first, second):
        return self.shift(first, second) if half == 0 else self.shift(second, first)

    def greet(self, far):
        barrier = pltpu.get_barrier_semaphore()
        steps = (1, 2, 3) if far else (1, 3)
        others = [{"feat": self.peer(step)} for step in range(1, FEATS)]
        others += [{"node": self.shift(step, 0)} for step in steps]
        others += [{"node": self.shift(0, step)} for step in steps]
        for other in others:
            pl.semaphore_signal(barrier, inc=1, device_id=other, device_id_type=MESH)
        pl.semaphore_wait(barrier, len(others))


class Copies:
    def __init__(self):
        self.sent = []

    def send(self, source, target, send_sem, recv_sem, device):
        copy = pltpu.make_async_remote_copy(
            src_ref=source,
            dst_ref=target,
            send_sem=send_sem,
            recv_sem=recv_sem,
            device_id=device,
            device_id_type=MESH,
        )
        copy.start()
        self.sent.append(copy)
        return copy

    def finish(self):
        for copy in self.sent:
            copy.wait_send()


class Regroup:
    def __init__(self, copies, place, source_at, target_at, send_sems, recv_sems):
        self.place, self.source_at, self.target_at = place, source_at, target_at
        self.parts = []
        for step in range(1, FEATS):
            to = place.peer(step)
            self.parts.append(
                copies.send(
                    source_at(to),
                    target_at(place.feat),
                    send_sems.at[step - 1],
                    recv_sems.at[step - 1],
                    {"feat": to},
                )
            )
        target_at(place.feat)[...] = source_at(place.feat)[...]

    def wait(self):
        for part in self.parts:
            part.wait_recv()


class Gather:
    def __init__(self, copies, place, own, out, send_sems, recv_sems):
        self.copies, self.place, self.own, self.out = copies, place, own, out
        self.send_sems, self.recv_sems = send_sems, recv_sems
        self.made = {}

    def _send(self, half, unit, role, source, target, first, second):
        place = self.place
        self.made[half, unit, role] = self.copies.send(
            source,
            target,
            self.send_sems.at[half, unit, role],
            self.recv_sems.at[half, unit, role],
            {"node": place.turned(half, first, second)},
        )

    def full(self, half, unit):
        rows = pl.ds(half * HALF, HALF)
        ahead = 0 if unit == SIDE else AHEAD[unit]
        shard = self.place.turned(half, ahead, 0)
        source = self.own.at[rows] if ahead == 0 else self.out.at[shard, rows]
        for role, way in ((0, 1), (1, -1)):
            move = (way, 0) if unit == SIDE else (0, way)
            self._send(half, unit, role, source, self.out.at[shard, rows], *move)

    def forward(self, half, unit, role):
        way = 1 if role == 0 else -1
        self.made[half, unit, role].wait_recv()
        rows = pl.ds(half * HALF + role * QUARTER, QUARTER)
        if unit == SIDE:
            shard, move = self.place.turned(half, -way, 0), (way, 0)
        else:
            shard, move = self.place.turned(half, AHEAD[unit], -way), (0, way)
        part = self.out.at[shard, rows]
        self._send(half, unit, role + 2, part, part, *move)

    def arrived(self, half, unit):
        for role in (2, 3):
            self.made[half, unit, role].wait_recv()

    def start(self):
        for half in range(2):
            self.full(half, SIDE)
        for half in range(2):
            self.full(half, 0)

    def rows(self):
        for role in range(2):
            for half in range(2):
                self.forward(half, SIDE, role)
                self.full(half, role + 1)

    def near(self):
        for role in range(2):
            for half in range(2):
                self.forward(half, 0, role)
        for half in range(2):
            self.arrived(half, SIDE)
            self.full(half, 3)

    def far(self):
        for unit in range(1, SIDE):
            for role in range(2):
                for half in range(2):
                    self.forward(half, unit, role)

    def last(self):
        for unit in range(SIDE):
            for half in range(2):
                self.arrived(half, unit)


class Scatter:
    def __init__(self, copies, place, parts, bufs, send_sems, recv_sems):
        self.copies, self.place, self.parts = copies, place, parts
        self.pass1, self.got1, self.sum1, self.half1, self.pass2, self.got2, self.sum2 = bufs
        self.send_sems, self.recv_sems = send_sems, recv_sems
        self.made = {}

    def _send(self, half, phase, side, kind, source, target):
        way = 1 if side == 0 else -1
        first, second = (way, 0) if phase == 0 else (0, way)
        self.made[half, phase, side, kind] = self.copies.send(
            source,
            target,
            self.send_sems.at[half, phase, side, kind],
            self.recv_sems.at[half, phase, side, kind],
            {"node": self.place.turned(half, first, second)},
        )

    def _line(self, half, ahead, quarter=None):
        rows = pl.ds(half * HALF, HALF)
        if quarter is not None:
            rows = pl.ds(half * HALF + quarter * QUARTER, QUARTER)
        if half == 0:
            return self.parts.at[(self.place.x + ahead + SIDE) % SIDE, :, rows]
        return self.parts.at[:, (self.place.z + ahead + SIDE) % SIDE, rows]

    def _unit(self, half, ahead, quarter):
        at = self.place.z if half == 0 else self.place.x
        rows = pl.ds(quarter * QUARTER, QUARTER)
        return self.half1.at[half, (at + ahead + SIDE) % SIDE, rows]

    def start(self):
        for half in range(2):
            for side, way in ((0, 1), (1, -1)):
                self._send(half, 0, side, 0, self._line(half, 2 * way, side), self.pass1.at[half, side])
        for half in range(2):
            for side, way in ((0, 1), (1, -1)):
                rows = pl.ds((1 - side) * QUARTER, QUARTER)
                self._send(half, 0, side, 1, self._line(half, way, 1 - side), self.got1.at[half, side, :, rows])

    def middle(self):
        for side, way in ((0, 1), (1, -1)):
            for half in range(2):
                self.made[half, 0, side, 0].wait_recv()
                mine, came, total = self._line(half, way, side), self.pass1.at[half, side], self.sum1.at[half, side]

                @pl.loop(0, SIDE)
                def _(shard):
                    total[shard] = (mine[shard].astype(F32) + came[shard].astype(F32)).astype(BF16)

                rows = pl.ds(side * QUARTER, QUARTER)
                self._send(half, 0, side, 2, total, self.got1.at[half, side, :, rows])

    def turn(self):
        for half in range(2):
            for side in range(2):
                for kind in (1, 2):
                    self.made[half, 0, side, kind].wait_recv()
            mine, left, right, total = self._line(half, 0), self.got1.at[half, 0], self.got1.at[half, 1], self.half1.at[half]

            @pl.loop(0, SIDE)
            def _(shard):
                near = left[shard].astype(F32) + right[shard].astype(F32)
                total[shard] = (mine[shard].astype(F32) + near).astype(BF16)

            for side, way in ((0, 1), (1, -1)):
                self._send(half, 1, side, 0, self._unit(half, 2 * way, side), self.pass2.at[half, side])
            for side, way in ((0, 1), (1, -1)):
                rows = pl.ds((1 - side) * QUARTER, QUARTER)
                self._send(half, 1, side, 1, self._unit(half, way, 1 - side), self.got2.at[half, side, rows])

    def middle2(self):
        for side, way in ((0, 1), (1, -1)):
            for half in range(2):
                self.made[half, 1, side, 0].wait_recv()
                total = self.sum2.at[half, side]
                mine, came = self._unit(half, way, side)[...], self.pass2[half, side]
                total[...] = (mine.astype(F32) + came.astype(F32)).astype(BF16)
                rows = pl.ds(side * QUARTER, QUARTER)
                self._send(half, 1, side, 2, total, self.got2.at[half, side, rows])

    def end(self, out):
        for half in range(2):
            for side in range(2):
                for kind in (1, 2):
                    self.made[half, 1, side, kind].wait_recv()
            for quarter in range(2):
                rows = pl.ds(quarter * QUARTER, QUARTER)
                near = self.got2[half, 0, rows].astype(F32) + self.got2[half, 1, rows].astype(F32)
                total = self._unit(half, 0, quarter)[...].astype(F32) + near
                out[pl.ds(half * HALF + quarter * QUARTER, QUARTER)] = total.astype(BF16)


class Total:
    def __init__(self, copies, place, part, feat_buf, x_buf, z_buf, send_sems, recv_sems):
        self.copies, self.place, self.part = copies, place, part
        self.bufs = (feat_buf, x_buf, z_buf)
        self.sems = (send_sems, recv_sems)

    def over_feat(self):
        buf = self.bufs[0]
        sends, recvs = self.sems
        self.regroup = Regroup(
            self.copies,
            self.place,
            lambda to: self.part.at[to],
            lambda slot: buf.at[slot],
            sends.at[pl.ds(0, FEATS - 1)],
            recvs.at[pl.ds(0, FEATS - 1)],
        )

    def _spread(self, axis, value):
        buf, place = self.bufs[1 + axis], self.place
        sends, recvs = self.sems
        at = place.x if axis == 0 else place.z
        buf[at] = value
        self.parts = []
        for step in range(1, SIDE):
            slot = FEATS - 1 + axis * (SIDE - 1) + step - 1
            to = place.shift(step, 0) if axis == 0 else place.shift(0, step)
            self.parts.append(
                self.copies.send(buf.at[at], buf.at[at], sends.at[slot], recvs.at[slot], {"node": to})
            )

    def over_x(self):
        self.regroup.wait()
        self._spread(0, sum(self.bufs[0][slot] for slot in range(FEATS)))

    def over_z(self):
        for part in self.parts:
            part.wait_recv()
        self._spread(1, sum(self.bufs[1][slot] for slot in range(SIDE)))

    def end(self):
        for part in self.parts:
            part.wait_recv()
        return sum(self.bufs[2][slot] for slot in range(SIDE))


def own_rows(feat):
    return pl.ds(feat * OWN, OWN)


def gather_kernel(
    features, weights1, weights2, cotangent, degrees,
    all_feats, own_feats, all_weights1, all_weights2, spread,
    blocks, outgoing, gather_send, gather_recv, feat_send, feat_recv, local_sem,
):
    place, copies = Place(), Copies()
    place.greet(False)
    regroups = [
        Regroup(
            copies, place, lambda to: weights, lambda slot: target.at[slot], feat_send.at[number], feat_recv.at[number]
        )
        for number, (weights, target) in enumerate(((weights2, all_weights2), (weights1, all_weights1)))
    ]
    for block in range(NB):
        blocks[block] = features[:, block * BLK : (block + 1) * BLK]
    gather = Gather(copies, place, blocks, all_feats, gather_send, gather_recv)
    gather.start()
    own = pltpu.make_async_copy(blocks, all_feats.at[place.node], local_sem)
    own.start()
    regroups.append(
        Regroup(
            copies, place, lambda to: blocks.at[own_rows(to)], lambda slot: own_feats.at[slot], feat_send.at[2], feat_recv.at[2]
        )
    )
    gather.rows()
    regroups[0].wait()
    neighbour = all_weights2[:, 1].reshape(-1, all_weights2.shape[-1])
    for block in range(OWN):
        nodes = cotangent[block * BLK : (block + 1) * BLK, :]
        back = dot(neighbour, nodes, ((1,), (1,)))
        degree = degrees[pl.ds(place.feat * OWN + block, 1), :].astype(F32)
        outgoing[:, block] = (back / degree).astype(BF16).reshape(FEATS, -1, BLK)
    regroups.append(
        Regroup(
            copies, place, lambda to: outgoing.at[to], lambda slot: spread.at[slot], feat_send.at[3], feat_recv.at[3]
        )
    )
    gather.near()
    gather.far()
    for regroup in regroups[1:]:
        regroup.wait()
    gather.last()
    own.wait()
    copies.finish()


def plan_groups(counts, groups):
    def row(block, total):
        for part in range(4):
            groups[total + part] = block * 4 + part
        return total + (counts[block] + GROUP - 1) // GROUP

    total = lax.fori_loop(0, NB, row, jnp.int32(0))
    for part in range(BATCH):
        groups[total + part] = 0
    return total


def each_step(counts, groups, tiles, held, tile_sems, work):
    total = plan_groups(counts, groups)
    steps = (total + BATCH - 1) // BATCH

    def copy(step, place):
        slot = step % STAGES
        group = groups[step * BATCH + place]
        return pltpu.make_async_copy(tiles.at[group], held.at[slot, place], tile_sems.at[slot, place])

    def fetch(step):
        @pl.when(step < steps)
        def _():
            for place in range(BATCH):
                copy(step, place).start()

    for step in range(STAGES - 1):
        fetch(step)

    def body(step, carry):
        fetch(step + STAGES - 1)
        entries = []
        for place in range(BATCH):
            copy(step, place).wait()
            group = groups[step * BATCH + place]
            block, first = group // 4, (group % 4) * GROUP
            live = jnp.where(step * BATCH + place < total, counts[block], 0)
            wide = jnp.concatenate([held[step % STAGES, place, slot] for slot in range(GROUP)], axis=1)
            entries.append((block, first, live, wide))
        work(entries)
        return carry

    lax.fori_loop(0, steps, body, jnp.int32(0))


def picked(source, cols, entry):
    block, first, live, wide = entry
    parts = []
    for slot in range(GROUP):
        value = source[cols[block, first + slot]]
        parts.append(jnp.where(first + slot < live, value, jnp.zeros_like(value)))
    return dot(jnp.concatenate(parts, axis=1), wide, ((1,), (1,)))


def write_mean(sums, degrees, mean):
    @pl.loop(0, NB)
    def _(block):
        mean[block] = (sums[block] / degrees[pl.ds(block, 1), :].astype(F32)).astype(BF16)


def both_kernel(cols, counts, tiles, source, spread, degrees, mean, back, held, sums, back_sums, groups, tile_sems):
    sums[...] = jnp.zeros_like(sums)

    @pl.loop(0, back_sums.shape[0] // 16)
    def _(part):
        rows = pl.ds(part * 16, 16)
        back_sums[rows] = jnp.zeros((16,) + back_sums.shape[1:], F32)

    def work(entries):
        products = [picked(source, cols, entry) for entry in entries]
        backs = [dot(spread[entry[0]], entry[3], ((1,), (0,))) for entry in entries]
        for entry, product in zip(entries, products):
            sums[entry[0]] += product
        for (block, first, live, _), product in zip(entries, backs):
            for slot in range(GROUP):
                part = product[:, slot * BLK : (slot + 1) * BLK]
                back_sums[cols[block, first + slot]] += jnp.where(first + slot < live, part, jnp.zeros_like(part))

    each_step(counts, groups, tiles, held, tile_sems, work)
    write_mean(sums, degrees, mean)

    @pl.loop(0, back_sums.shape[0] // 16)
    def _(part):
        rows = pl.ds(part * 16, 16)
        back[rows] = back_sums[rows].astype(BF16)


def mean_kernel(cols, counts, tiles, source, degrees, mean, held, sums, groups, tile_sems):
    sums[...] = jnp.zeros_like(sums)

    def work(entries):
        products = [picked(source, cols, entry) for entry in entries]
        for entry, product in zip(entries, products):
            sums[entry[0]] += product

    each_step(counts, groups, tiles, held, tile_sems, work)
    write_mean(sums, degrees, mean)


def middle_kernel(
    scale, feat_mean, back_parts, own_feats, weights1, bias1, weights2, cotangent,
    all_hidden, hidden, grad_first,
    means, slopes, own_hidden, back, own_back, grads, feat_buf, x_buf, z_buf, bufs,
    gather_send, gather_recv, scatter_send, scatter_recv, feat_send, feat_recv, total_send, total_recv, local_sem,
):
    place, copies = Place(), Copies()
    place.greet(True)
    to_means = Regroup(
        copies, place, lambda to: feat_mean.at[own_rows(to)], lambda slot: means.at[slot], feat_send.at[0], feat_recv.at[0]
    )
    scatter = Scatter(copies, place, back_parts, bufs, scatter_send, scatter_recv)
    scatter.start()
    width = weights1.shape[-1]
    first = weights1[...].reshape(-1, width)
    to_means.wait()

    def stack(block):
        parts = []
        for part in range(FEATS):
            parts += [own_feats[part, block], means[part, block]]
        return jnp.concatenate(parts, axis=0)

    for block in range(OWN):
        pre = dot(first, stack(block), ((0,), (0,))) + bias1[...]
        sigmoid = jax.nn.sigmoid(pre)
        slopes[block] = (sigmoid * (1.0 + pre * (1.0 - sigmoid))).astype(BF16)
        hidden[:, block] = (pre * sigmoid).astype(BF16).reshape(FEATS, -1, BLK)
    to_hidden = Regroup(
        copies, place, lambda to: hidden.at[to], lambda slot: own_hidden.at[own_rows(slot)], feat_send.at[1], feat_recv.at[1]
    )
    scatter.middle()
    to_hidden.wait()
    gather = Gather(copies, place, own_hidden, all_hidden, gather_send, gather_recv)
    own = pltpu.make_async_copy(own_hidden, all_hidden.at[place.node], local_sem)
    own.start()
    scatter.turn()
    gather.start()
    scatter.middle2()
    gather.rows()
    scatter.end(back)
    to_back = Regroup(
        copies, place, lambda to: back.at[own_rows(to)], lambda slot: own_back.at[slot], feat_send.at[2], feat_recv.at[2]
    )
    gather.near()
    to_back.wait()
    own_weights = weights2[:, 0].reshape(-1, weights2.shape[-1])
    total = None
    for block in range(OWN):
        nodes = cotangent[block * BLK : (block + 1) * BLK, :]
        came = jnp.concatenate([own_back[part, block] for part in range(FEATS)], axis=0)
        grad = dot(own_weights, nodes, ((1,), (1,))) + came.astype(F32)
        grad = (grad * slopes[block].astype(F32)).astype(BF16)
        product = dot(stack(block), grad, ((1,), (1,)))
        total = product if total is None else total + product
    grads[...] = total.reshape(grads.shape)
    summed = Total(copies, place, grads, feat_buf, x_buf, z_buf, total_send, total_recv)
    summed.over_feat()
    gather.far()
    summed.over_x()
    summed.over_z()
    grad_first[...] = summed.end() * scale
    gather.last()
    own.wait()
    copies.finish()


def last_kernel(
    scale, hidden_mean, hidden, weights2, bias2, cotangent,
    hidden_out, grad_second,
    means, grads, feat_buf, x_buf, z_buf, feat_send, feat_recv, total_send, total_recv,
):
    place, copies = Place(), Copies()
    place.greet(True)
    to_means = Regroup(
        copies, place, lambda to: hidden_mean.at[own_rows(to)], lambda slot: means.at[slot], feat_send, feat_recv
    )
    second = weights2[...].reshape(-1, weights2.shape[-1])
    to_means.wait()

    def stack(block):
        parts = []
        for part in range(FEATS):
            parts += [hidden[part, block], means[part, block]]
        return jnp.concatenate(parts, axis=0)

    total = None
    for block in range(OWN):
        nodes = cotangent[block * BLK : (block + 1) * BLK, :]
        product = dot(stack(block), nodes, ((1,), (0,)))
        total = product if total is None else total + product
    grads[...] = total.reshape(grads.shape)
    summed = Total(copies, place, grads, feat_buf, x_buf, z_buf, total_send, total_recv)
    summed.over_feat()
    for block in range(OWN):
        out = dot(stack(block), second, ((0,), (0,))) + bias2[...]
        hidden_out[block * BLK : (block + 1) * BLK, :] = out.astype(BF16)
    summed.over_x()
    summed.over_z()
    grad_second[...] = summed.end() * scale
    copies.finish()


def remote(collective_id):
    return pltpu.CompilerParams(
        collective_id=collective_id, has_side_effects=True, vmem_limit_bytes=44 * 1024 * 1024
    )


def shape(*dims, dtype=BF16):
    return jax.ShapeDtypeStruct(dims, dtype)


def buf(*dims, dtype=BF16):
    return pltpu.VMEM(dims, dtype)


def dma(*dims):
    return pltpu.SemaphoreType.DMA(dims)


def shards(
    features, tile_cols, tile_counts, tiles, degrees, weights1, bias1, weights2, bias2, cotangent
):
    feat_part = features.shape[0]
    hid_part = weights2.shape[1]
    width = weights2.shape[2]
    shard_total = lax.axis_size("node")
    block_total = shard_total * NB
    scale = 1.0 / math.sqrt(features.shape[1] * shard_total)
    own_nodes = OWN * BLK
    degree_rows = degrees.reshape(NB, BLK)
    groups = tiles.reshape(NB * tiles.shape[1] // GROUP, GROUP, BLK, BLK)

    all_feats, own_feats, all_weights1, all_weights2, spread = pl.pallas_call(
        gather_kernel,
        out_shape=(
            shape(shard_total, NB, feat_part, BLK),
            shape(FEATS, OWN, feat_part, BLK),
            shape(FEATS, 2, feat_part, width),
            shape(FEATS, 2, hid_part, width),
            shape(FEATS, OWN, hid_part, BLK),
        ),
        in_specs=[VMEM] * 5,
        out_specs=(ANY, VMEM, VMEM, VMEM, VMEM),
        scratch_shapes=[
            buf(NB, feat_part, BLK),
            buf(FEATS, OWN, hid_part, BLK),
            dma(2, 5, 4),
            dma(2, 5, 4),
            dma(4, FEATS - 1),
            dma(4, FEATS - 1),
            pltpu.SemaphoreType.DMA,
        ],
        compiler_params=remote(1),
        name="gather_features",
    )(features, weights1, weights2, cotangent, degree_rows)

    held = buf(STAGES, BATCH, GROUP, BLK, BLK)
    listed = pltpu.SMEM((NB * 4 + 2 * BATCH,), jnp.int32)
    plain = pltpu.CompilerParams(vmem_limit_bytes=52 * 1024 * 1024)
    feat_mean, back_parts = pl.pallas_call(
        both_kernel,
        out_shape=(shape(NB, feat_part, BLK), shape(block_total, hid_part, BLK)),
        in_specs=[SMEM, SMEM, ANY, VMEM, VMEM, VMEM],
        out_specs=(VMEM, VMEM),
        scratch_shapes=[
            held,
            buf(NB, feat_part, BLK, dtype=F32),
            buf(block_total, hid_part, BLK, dtype=F32),
            listed,
            dma(STAGES, BATCH),
        ],
        compiler_params=plain,
        name="aggregate_both",
    )(
        tile_cols,
        tile_counts,
        groups,
        all_feats.reshape(block_total, feat_part, BLK),
        spread.reshape(NB, hid_part, BLK),
        degree_rows,
    )

    row = (SIDE, HALF, hid_part, BLK)
    part_row = (SIDE, QUARTER, hid_part, BLK)
    middle_bufs = (
        buf(2, 2, *part_row),
        buf(2, 2, *row),
        buf(2, 2, *part_row),
        buf(2, *row),
        buf(2, 2, *part_row[1:]),
        buf(2, 2, *row[1:]),
        buf(2, 2, *part_row[1:]),
    )
    first_rows = 2 * feat_part
    all_hidden, hidden, grad_first = pl.pallas_call(
        functools.partial(middle_kernel, scale),
        out_shape=(
            shape(shard_total, NB, hid_part, BLK),
            shape(FEATS, OWN, hid_part, BLK),
            shape(first_rows, width, dtype=F32),
        ),
        in_specs=[VMEM] * 7,
        out_specs=(ANY, VMEM, VMEM),
        scratch_shapes=[
            buf(FEATS, OWN, feat_part, BLK),
            buf(OWN, width, BLK),
            buf(NB, hid_part, BLK),
            buf(NB, hid_part, BLK),
            buf(FEATS, OWN, hid_part, BLK),
            buf(FEATS, first_rows, width, dtype=F32),
            buf(FEATS, first_rows, width, dtype=F32),
            buf(SIDE, first_rows, width, dtype=F32),
            buf(SIDE, first_rows, width, dtype=F32),
            middle_bufs,
            dma(2, 5, 4),
            dma(2, 5, 4),
            dma(2, 2, 2, 3),
            dma(2, 2, 2, 3),
            dma(3, FEATS - 1),
            dma(3, FEATS - 1),
            dma(FEATS - 1 + 2 * (SIDE - 1)),
            dma(FEATS - 1 + 2 * (SIDE - 1)),
            pltpu.SemaphoreType.DMA,
        ],
        compiler_params=remote(2),
        name="first_layer",
    )(
        feat_mean,
        back_parts.reshape(SIDE, SIDE, NB, hid_part, BLK),
        own_feats,
        all_weights1,
        bias1.reshape(width, 1),
        all_weights2,
        cotangent,
    )

    hidden_mean = pl.pallas_call(
        mean_kernel,
        out_shape=shape(NB, hid_part, BLK),
        in_specs=[SMEM, SMEM, ANY, VMEM, VMEM],
        out_specs=VMEM,
        scratch_shapes=[held, buf(NB, hid_part, BLK, dtype=F32), listed, dma(STAGES, BATCH)],
        compiler_params=plain,
        name="aggregate_hidden",
    )(tile_cols, tile_counts, groups, all_hidden.reshape(block_total, hid_part, BLK), degree_rows)

    second_rows = 2 * hid_part
    hidden_out, grad_second = pl.pallas_call(
        functools.partial(last_kernel, scale),
        out_shape=(shape(own_nodes, width), shape(second_rows, width, dtype=F32)),
        in_specs=[VMEM] * 5,
        out_specs=(VMEM, VMEM),
        scratch_shapes=[
            buf(FEATS, OWN, hid_part, BLK),
            buf(FEATS, second_rows, width, dtype=F32),
            buf(FEATS, second_rows, width, dtype=F32),
            buf(SIDE, second_rows, width, dtype=F32),
            buf(SIDE, second_rows, width, dtype=F32),
            dma(FEATS - 1),
            dma(FEATS - 1),
            dma(FEATS - 1 + 2 * (SIDE - 1)),
            dma(FEATS - 1 + 2 * (SIDE - 1)),
        ],
        compiler_params=remote(3),
        name="second_layer",
    )(hidden_mean, hidden, all_weights2, bias2.reshape(1, width), cotangent)
    return (
        hidden_out,
        grad_second.reshape(2, hid_part, width),
        grad_first.reshape(2, feat_part, width),
    )


def solution(mesh):
    return jax.shard_map(
        shards,
        mesh=mesh,
        in_specs=(
            P("feat", "node"),
            P("node", None),
            P("node"),
            P("node", None, None, None),
            P("node"),
            P(None, "feat", None),
            P(),
            P(None, "feat", None),
            P(),
            P(("node", "feat"), None),
        ),
        out_specs=(P(("node", "feat"), None), P(None, "feat", None), P(None, "feat", None)),
        check_vma=False,
    )
```

```python
import functools
import math

import jax
import jax.numpy as jnp
from jax import lax
from jax.experimental import pallas as pl
from jax.experimental.pallas import tpu as pltpu
from jax.sharding import PartitionSpec as P

MESH = pl.DeviceIdType.MESH
BF16 = jnp.bfloat16
F32 = jnp.float32
FEATS = 8
SIDE = 4
BLK = 128
NB = 48
OWN = NB // FEATS
HALF, QUARTER = NB // 2, NB // 4
GROUP = 4
BATCH = 8
STAGES = 4
AHEAD = (0, -1, 1, 2)
VMEM = pl.BlockSpec(memory_space=pltpu.VMEM)
SMEM = pl.BlockSpec(memory_space=pltpu.SMEM)
ANY = pl.BlockSpec(memory_space=pl.ANY)
HBM = pl.BlockSpec(memory_space=pltpu.HBM)


def dot(left, right, dims):
    return lax.dot_general(left, right, (dims, ((), ())), preferred_element_type=F32)


class Place:
    def __init__(self):
        self.feat = lax.axis_index("feat")
        self.node = lax.axis_index("node")
        self.x = self.node // SIDE
        self.z = self.node % SIDE

    def peer(self, step):
        return (self.feat + step) % FEATS

    def shift(self, dx, dz):
        return ((self.x + dx + SIDE) % SIDE) * SIDE + (self.z + dz + SIDE) % SIDE

    def beside(self):
        return [self.shift(dx, dz) for dx, dz in ((1, 0), (-1, 0), (0, 1), (0, -1))]

    def others(self):
        total = SIDE * SIDE
        return [(self.node + step) % total for step in range(1, total)]

    def turned(self, half, first, second):
        return self.shift(first, second) if half == 0 else self.shift(second, first)

    def greet(self, nodes):
        barrier = pltpu.get_barrier_semaphore()
        others = [{"feat": self.peer(step)} for step in range(1, FEATS)]
        others += [{"node": node} for node in nodes]
        for other in others:
            pl.semaphore_signal(barrier, inc=1, device_id=other, device_id_type=MESH)
        pl.semaphore_wait(barrier, len(others))


class Copies:
    def __init__(self):
        self.sent = []

    def send(self, source, target, send_sem, recv_sem, device):
        copy = pltpu.make_async_remote_copy(
            src_ref=source,
            dst_ref=target,
            send_sem=send_sem,
            recv_sem=recv_sem,
            device_id=device,
            device_id_type=MESH,
        )
        copy.start()
        self.sent.append(copy)
        return copy

    def finish(self):
        for copy in self.sent:
            copy.wait_send()


class Regroup:
    def __init__(self, copies, place, source_at, target_at, send_sems, recv_sems, own=True):
        self.parts = []
        for step in range(1, FEATS):
            to = place.peer(step)
            self.parts.append(
                copies.send(
                    source_at(to),
                    target_at(place.feat),
                    send_sems.at[step - 1],
                    recv_sems.at[step - 1],
                    {"feat": to},
                )
            )
        if own:
            target_at(place.feat)[...] = source_at(place.feat)[...]

    def wait(self):
        for part in self.parts:
            part.wait_recv()


class Gather:
    def __init__(self, copies, place, own, out, send_sems, recv_sems):
        self.copies, self.place, self.own, self.out = copies, place, own, out
        self.send_sems, self.recv_sems = send_sems, recv_sems
        self.made = {}

    def _send(self, half, unit, role, source, target, first, second):
        place = self.place
        self.made[half, unit, role] = self.copies.send(
            source,
            target,
            self.send_sems.at[half, unit, role],
            self.recv_sems.at[half, unit, role],
            {"node": place.turned(half, first, second)},
        )

    def full(self, half, unit):
        rows = pl.ds(half * HALF, HALF)
        ahead = 0 if unit == SIDE else AHEAD[unit]
        shard = self.place.turned(half, ahead, 0)
        source = self.own.at[rows] if ahead == 0 else self.out.at[shard, rows]
        for role, way in ((0, 1), (1, -1)):
            move = (way, 0) if unit == SIDE else (0, way)
            self._send(half, unit, role, source, self.out.at[shard, rows], *move)

    def forward(self, half, unit, role):
        way = 1 if role == 0 else -1
        self.made[half, unit, role].wait_recv()
        rows = pl.ds(half * HALF + role * QUARTER, QUARTER)
        if unit == SIDE:
            shard, move = self.place.turned(half, -way, 0), (way, 0)
        else:
            shard, move = self.place.turned(half, AHEAD[unit], -way), (0, way)
        part = self.out.at[shard, rows]
        self._send(half, unit, role + 2, part, part, *move)

    def arrived(self, half, unit):
        for role in (2, 3):
            self.made[half, unit, role].wait_recv()

    def start(self):
        for half in range(2):
            self.full(half, SIDE)
        for half in range(2):
            self.full(half, 0)

    def rows(self):
        for role in range(2):
            for half in range(2):
                self.forward(half, SIDE, role)
                self.full(half, role + 1)

    def near(self):
        for role in range(2):
            for half in range(2):
                self.forward(half, 0, role)
        for half in range(2):
            self.arrived(half, SIDE)
            self.full(half, 3)

    def far(self, units=(1, 2, 3)):
        for unit in units:
            for role in range(2):
                for half in range(2):
                    self.forward(half, unit, role)

    def last(self):
        for unit in range(SIDE):
            for half in range(2):
                self.arrived(half, unit)


class Scatter:
    def __init__(self, copies, place, parts, bufs, send_sems, recv_sems):
        self.copies, self.place, self.parts = copies, place, parts
        self.pass1, self.got1, self.sum1, self.half1, self.pass2, self.got2, self.sum2 = bufs
        self.send_sems, self.recv_sems = send_sems, recv_sems
        self.made = {}

    def _send(self, half, phase, side, kind, source, target):
        way = 1 if side == 0 else -1
        first, second = (way, 0) if phase == 0 else (0, way)
        self.made[half, phase, side, kind] = self.copies.send(
            source,
            target,
            self.send_sems.at[half, phase, side, kind],
            self.recv_sems.at[half, phase, side, kind],
            {"node": self.place.turned(half, first, second)},
        )

    def _line(self, half, ahead, quarter=None):
        rows = pl.ds(half * HALF, HALF)
        if quarter is not None:
            rows = pl.ds(half * HALF + quarter * QUARTER, QUARTER)
        if half == 0:
            return self.parts.at[(self.place.x + ahead + SIDE) % SIDE, :, rows]
        return self.parts.at[:, (self.place.z + ahead + SIDE) % SIDE, rows]

    def _unit(self, half, ahead, quarter):
        at = self.place.z if half == 0 else self.place.x
        rows = pl.ds(quarter * QUARTER, QUARTER)
        return self.half1.at[half, (at + ahead + SIDE) % SIDE, rows]

    def start(self):
        for half in range(2):
            for side, way in ((0, 1), (1, -1)):
                self._send(half, 0, side, 0, self._line(half, 2 * way, side), self.pass1.at[half, side])
        for half in range(2):
            for side, way in ((0, 1), (1, -1)):
                rows = pl.ds((1 - side) * QUARTER, QUARTER)
                self._send(half, 0, side, 1, self._line(half, way, 1 - side), self.got1.at[half, side, :, rows])

    def middle(self):
        for side, way in ((0, 1), (1, -1)):
            for half in range(2):
                self.made[half, 0, side, 0].wait_recv()
                mine, came, total = self._line(half, way, side), self.pass1.at[half, side], self.sum1.at[half, side]

                @pl.loop(0, SIDE)
                def _(shard):
                    total[shard] = (mine[shard].astype(F32) + came[shard].astype(F32)).astype(BF16)

                rows = pl.ds(side * QUARTER, QUARTER)
                self._send(half, 0, side, 2, total, self.got1.at[half, side, :, rows])

    def turn(self):
        for half in range(2):
            for side in range(2):
                for kind in (1, 2):
                    self.made[half, 0, side, kind].wait_recv()
            mine, left, right, total = self._line(half, 0), self.got1.at[half, 0], self.got1.at[half, 1], self.half1.at[half]

            @pl.loop(0, SIDE)
            def _(shard):
                near = left[shard].astype(F32) + right[shard].astype(F32)
                total[shard] = (mine[shard].astype(F32) + near).astype(BF16)

            for side, way in ((0, 1), (1, -1)):
                self._send(half, 1, side, 0, self._unit(half, 2 * way, side), self.pass2.at[half, side])
            for side, way in ((0, 1), (1, -1)):
                rows = pl.ds((1 - side) * QUARTER, QUARTER)
                self._send(half, 1, side, 1, self._unit(half, way, 1 - side), self.got2.at[half, side, rows])

    def middle2(self):
        for side, way in ((0, 1), (1, -1)):
            for half in range(2):
                self.made[half, 1, side, 0].wait_recv()
                total = self.sum2.at[half, side]
                mine, came = self._unit(half, way, side)[...], self.pass2[half, side]
                total[...] = (mine.astype(F32) + came.astype(F32)).astype(BF16)
                rows = pl.ds(side * QUARTER, QUARTER)
                self._send(half, 1, side, 2, total, self.got2.at[half, side, rows])

    def end(self, out):
        for half in range(2):
            for side in range(2):
                for kind in (1, 2):
                    self.made[half, 1, side, kind].wait_recv()
            for quarter in range(2):
                rows = pl.ds(quarter * QUARTER, QUARTER)
                near = self.got2[half, 0, rows].astype(F32) + self.got2[half, 1, rows].astype(F32)
                total = self._unit(half, 0, quarter)[...].astype(F32) + near
                out[pl.ds(half * HALF + quarter * QUARTER, QUARTER)] = total.astype(BF16)


class Total:
    def __init__(self, copies, place, part, came, summed, send_sems, recv_sems):
        self.copies, self.place, self.part, self.came, self.summed = copies, place, part, came, summed
        self.send_sems, self.recv_sems = send_sems, recv_sems

    def _all(self, phase, source_at, target):
        place = self.place
        self.parts = []
        for number, node in enumerate(place.others()):
            self.parts.append(
                self.copies.send(
                    source_at(node),
                    target.at[place.node],
                    self.send_sems.at[phase, number],
                    self.recv_sems.at[phase, number],
                    {"node": node},
                )
            )

    def start(self):
        self._all(0, lambda node: self.part.at[node], self.came)
        self.came[self.place.node] = self.part[self.place.node]

    def turn(self):
        for part in self.parts:
            part.wait_recv()
        self.summed[self.place.node] = sum(self.came[slot] for slot in range(SIDE * SIDE))
        self._all(1, lambda node: self.summed.at[self.place.node], self.summed)

    def end(self):
        for part in self.parts:
            part.wait_recv()


def own_rows(feat):
    return pl.ds(feat * OWN, OWN)


def gather_kernel(
    features_in, weights1, weights2, cotangent_in, degrees_in,
    all_feats, own_feats, all_weights1, all_weights2, spread,
    features, cotangent, degrees, own_weights1, own_weights2, blocks, outgoing,
    gather_send, gather_recv, feat_send, feat_recv, local_sems,
):
    place, copies = Place(), Copies()
    pairs = (
        (features_in, features),
        (weights2, own_weights2),
        (weights1, own_weights1),
        (cotangent_in, cotangent),
        (degrees_in, degrees),
    )
    loads = [pltpu.make_async_copy(pair[0], pair[1], local_sems.at[number]) for number, pair in enumerate(pairs)]
    for load in loads:
        load.start()
    place.greet(place.beside())
    loads[0].wait()
    for block in range(NB):
        blocks[block] = features[:, block * BLK : (block + 1) * BLK]
    gather = Gather(copies, place, blocks, all_feats, gather_send, gather_recv)
    gather.start()
    regroups = []
    for number, (weights, target) in enumerate(((own_weights2, all_weights2), (own_weights1, all_weights1))):
        loads[1 + number].wait()
        regroups.append(
            Regroup(
                copies, place, lambda to: weights, lambda slot: target.at[slot], feat_send.at[number], feat_recv.at[number]
            )
        )
    own = pltpu.make_async_copy(blocks, all_feats.at[place.node], local_sems.at[len(pairs)])
    own.start()
    gather.rows()
    loads[3].wait()
    loads[4].wait()
    regroups[0].wait()
    neighbour = all_weights2[:, 1].reshape(-1, all_weights2.shape[-1])
    for block in range(OWN):
        nodes = cotangent[block * BLK : (block + 1) * BLK, :]
        back = dot(neighbour, nodes, ((1,), (1,)))
        degree = degrees[pl.ds(place.feat * OWN + block, 1), :].astype(F32)
        outgoing[:, block] = (back / degree).astype(BF16).reshape(FEATS, -1, BLK)
    regroups.append(
        Regroup(
            copies, place, lambda to: outgoing.at[to], lambda slot: spread.at[slot], feat_send.at[3], feat_recv.at[3]
        )
    )
    gather.near()
    regroups.append(
        Regroup(
            copies, place, lambda to: blocks.at[own_rows(to)], lambda slot: own_feats.at[slot], feat_send.at[2], feat_recv.at[2]
        )
    )
    gather.far()
    for regroup in regroups[1:]:
        regroup.wait()
    gather.last()
    own.wait()
    copies.finish()


def plan_groups(counts, groups):
    def row(block, total):
        for part in range(4):
            groups[total + part] = block * 4 + part
        return total + (counts[block] + GROUP - 1) // GROUP

    total = lax.fori_loop(0, NB, row, jnp.int32(0))
    for part in range(BATCH):
        groups[total + part] = 0
    return total


def each_step(counts, groups, tiles, held, tile_sems, work):
    total = plan_groups(counts, groups)
    steps = (total + BATCH - 1) // BATCH

    def copy(step, place):
        slot = step % STAGES
        group = groups[step * BATCH + place]
        return pltpu.make_async_copy(tiles.at[group], held.at[slot, place], tile_sems.at[slot, place])

    def fetch(step):
        @pl.when(step < steps)
        def _():
            for place in range(BATCH):
                copy(step, place).start()

    for step in range(STAGES - 1):
        fetch(step)

    def body(step, carry):
        fetch(step + STAGES - 1)
        entries = []
        for place in range(BATCH):
            copy(step, place).wait()
            group = groups[step * BATCH + place]
            block, first = group // 4, (group % 4) * GROUP
            live = jnp.where(step * BATCH + place < total, counts[block], 0)
            wide = jnp.concatenate([held[step % STAGES, place, slot] for slot in range(GROUP)], axis=1)
            entries.append((block, first, live, wide))
        work(entries)
        return carry

    lax.fori_loop(0, steps, body, jnp.int32(0))


def picked(source, cols, entry):
    block, first, live, wide = entry
    parts = []
    for slot in range(GROUP):
        value = source[cols[first + slot, block]]
        parts.append(jnp.where(first + slot < live, value, jnp.zeros_like(value)))
    return dot(jnp.concatenate(parts, axis=1), wide, ((1,), (1,)))


def write_mean(sums, degrees, mean):
    @pl.loop(0, NB)
    def _(block):
        mean[block] = (sums[block] / degrees[pl.ds(block, 1), :].astype(F32)).astype(BF16)


def both_kernel(cols, counts, tiles, source, spread, degrees, mean, back, held, sums, back_sums, groups, tile_sems):
    sums[...] = jnp.zeros_like(sums)

    @pl.loop(0, back_sums.shape[0] // 16)
    def _(part):
        rows = pl.ds(part * 16, 16)
        back_sums[rows] = jnp.zeros((16,) + back_sums.shape[1:], F32)

    def work(entries):
        products = [picked(source, cols, entry) for entry in entries]
        backs = [dot(spread[entry[0]], entry[3], ((1,), (0,))) for entry in entries]
        for entry, product in zip(entries, products):
            sums[entry[0]] += product
        for (block, first, live, _), product in zip(entries, backs):
            for slot in range(GROUP):
                part = product[:, slot * BLK : (slot + 1) * BLK]
                back_sums[cols[first + slot, block]] += jnp.where(first + slot < live, part, jnp.zeros_like(part))

    each_step(counts, groups, tiles, held, tile_sems, work)
    write_mean(sums, degrees, mean)

    @pl.loop(0, back_sums.shape[0] // 16)
    def _(part):
        rows = pl.ds(part * 16, 16)
        back[rows] = back_sums[rows].astype(BF16)


def mean_kernel(
    cols, counts, tiles, source, degrees, hidden, cotangent, mean, grads, held, sums, groups, tile_sems
):
    sums[...] = jnp.zeros_like(sums)

    def work(entries):
        products = [picked(source, cols, entry) for entry in entries]
        for entry, product in zip(entries, products):
            sums[entry[0]] += product

    each_step(counts, groups, tiles, held, tile_sems, work)
    write_mean(sums, degrees, mean)
    wide = 8
    total = jnp.zeros((2 * hidden.shape[1], cotangent.shape[-1]), F32)

    def add(part, total):
        blocks = [part * wide + block for block in range(wide)]
        stack = [jnp.concatenate([hidden[block], mean[block]], axis=0) for block in blocks]
        nodes = cotangent[pl.ds(part * wide, wide)].reshape(wide * BLK, -1)
        return total + dot(jnp.concatenate(stack, axis=1), nodes, ((1,), (0,)))

    put_tiles(grads, lax.fori_loop(0, NB // wide, add, total))


def put_tiles(out, value):
    for tile in range(out.shape[0]):
        out[tile] = value[tile // 2 * 8 : tile // 2 * 8 + 8, tile % 2 * BLK : tile % 2 * BLK + BLK]


def middle_kernel(
    feat_mean, back_parts, own_feats, weights1, bias1, weights2, cotangent_in,
    all_hidden, hidden, own_hidden, all_cotangent, grad_first,
    cotangent, means, slopes, back, own_back, grads, feat_buf, bufs,
    gather_send, gather_recv, scatter_send, scatter_recv, feat_send, feat_recv, local_sems,
):
    place, copies = Place(), Copies()
    load = pltpu.make_async_copy(cotangent_in, cotangent, local_sems.at[0])
    load.start()
    place.greet(place.beside())

    def regroup(number, source_at, target_at, own=True):
        return Regroup(copies, place, source_at, target_at, feat_send.at[number], feat_recv.at[number], own)

    to_means = regroup(0, lambda to: feat_mean.at[own_rows(to)], lambda slot: means.at[slot])
    scatter = Scatter(copies, place, back_parts, bufs, scatter_send, scatter_recv)
    scatter.start()
    first = weights1[...].reshape(-1, weights1.shape[-1])
    bias = jnp.transpose(jnp.broadcast_to(bias1[...], (BLK, bias1.shape[1])))
    to_means.wait()

    def stack(block):
        parts = []
        for part in range(FEATS):
            parts += [own_feats[part, block], means[part, block]]
        return jnp.concatenate(parts, axis=0)

    for block in range(OWN):
        pre = dot(first, stack(block), ((0,), (0,))) + bias
        sigmoid = jax.nn.sigmoid(pre)
        slopes[block] = (sigmoid * (1.0 + pre * (1.0 - sigmoid))).astype(BF16)
        hidden[:, block] = (pre * sigmoid).astype(BF16).reshape(FEATS, -1, BLK)
    to_hidden = regroup(1, lambda to: hidden.at[to], lambda slot: own_hidden.at[own_rows(slot)])
    scatter.middle()
    to_hidden.wait()
    gather = Gather(copies, place, own_hidden, all_hidden, gather_send, gather_recv)
    gather.start()
    own = pltpu.make_async_copy(own_hidden, all_hidden.at[place.node], local_sems.at[1])
    own.start()
    load.wait()
    to_cotangent = regroup(4, lambda to: cotangent, lambda slot: all_cotangent.at[slot], False)
    own_cotangent = pltpu.make_async_copy(cotangent, all_cotangent.at[place.feat], local_sems.at[2])
    own_cotangent.start()
    scatter.turn()
    gather.rows()
    scatter.middle2()
    gather.near()
    scatter.end(back)
    to_back = regroup(2, lambda to: back.at[own_rows(to)], lambda slot: own_back.at[slot])
    gather.far((1,))
    to_back.wait()
    own_weights = weights2[:, 0].reshape(-1, weights2.shape[-1])
    total = None
    for block in range(OWN):
        nodes = cotangent[block * BLK : (block + 1) * BLK, :]
        came = jnp.concatenate([own_back[part, block] for part in range(FEATS)], axis=0)
        grad = dot(own_weights, nodes, ((1,), (1,))) + came.astype(F32)
        grad = (grad * slopes[block].astype(F32)).astype(BF16)
        product = dot(stack(block), grad, ((1,), (1,)))
        total = product if total is None else total + product
    grads[...] = total.reshape(grads.shape)
    to_total = regroup(3, lambda to: grads.at[to], lambda slot: feat_buf.at[slot])
    gather.far((2, 3))
    to_total.wait()
    put_tiles(grad_first, sum(feat_buf[slot] for slot in range(FEATS)))
    gather.last()
    to_cotangent.wait()
    own_cotangent.wait()
    own.wait()
    copies.finish()


def last_kernel(
    hidden_mean, grad_first, grad_second,
    means, summed,
    part, came, feat_send, feat_recv, total_send, total_recv,
):
    place, copies = Place(), Copies()
    place.greet(place.others())
    to_means = Regroup(
        copies, place, lambda to: hidden_mean.at[own_rows(to)], lambda slot: means.at[slot], feat_send, feat_recv
    )
    part[:, 1] = jnp.zeros_like(part[:, 1])
    part[:, 0] = grad_second[...]
    part[pl.ds(0, grad_first.shape[0]), 1] = grad_first[...]
    total = Total(copies, place, part, came, summed, total_send, total_recv)
    total.start()
    total.turn()
    total.end()
    to_means.wait()
    copies.finish()


def out_kernel(scale, hidden, means, weights2, bias2, summed, hidden_out, grad_second, grad_first):
    second = weights2[...].reshape(-1, weights2.shape[-1])
    for block in range(OWN):
        parts = []
        for part in range(FEATS):
            parts += [hidden[part, block], means[part, block]]
        out = dot(jnp.concatenate(parts, axis=0), second, ((0,), (0,))) + bias2[...]
        hidden_out[block * BLK : (block + 1) * BLK, :] = out.astype(BF16)
    for kind, grad in enumerate((grad_second, grad_first)):
        for tile in range(grad.shape[0] // 8 * 2):
            rows, columns = pl.ds(tile // 2 * 8, 8), pl.ds(tile % 2 * BLK, BLK)
            grad[rows, columns] = summed[tile, kind] * scale


def limit(mib, collective_id=None):
    if collective_id is None:
        return pltpu.CompilerParams(vmem_limit_bytes=mib * 1024 * 1024)
    return pltpu.CompilerParams(
        collective_id=collective_id, has_side_effects=True, vmem_limit_bytes=mib * 1024 * 1024
    )


def shape(*dims, dtype=BF16):
    return jax.ShapeDtypeStruct(dims, dtype)


def buf(*dims, dtype=BF16):
    return pltpu.VMEM(dims, dtype)


def dma(*dims):
    return pltpu.SemaphoreType.DMA(dims)


def shards(
    features, tile_cols, tile_counts, tiles, degrees, weights1, bias1, weights2, bias2, cotangent
):
    feat_part = features.shape[0]
    hid_part = weights2.shape[1]
    width = weights2.shape[2]
    shard_total = lax.axis_size("node")
    block_total = shard_total * NB
    scale = 1.0 / math.sqrt(features.shape[1] * shard_total)
    own_nodes = OWN * BLK
    degree_rows = degrees.reshape(NB, BLK)
    groups = tiles.reshape(NB * tiles.shape[1] // GROUP, GROUP, BLK, BLK)

    all_feats, own_feats, all_weights1, all_weights2, spread = pl.pallas_call(
        gather_kernel,
        out_shape=(
            shape(shard_total, NB, feat_part, BLK),
            shape(FEATS, OWN, feat_part, BLK),
            shape(FEATS, 2, feat_part, width),
            shape(FEATS, 2, hid_part, width),
            shape(FEATS, OWN, hid_part, BLK),
        ),
        in_specs=[HBM] * 5,
        out_specs=(ANY, VMEM, VMEM, VMEM, VMEM),
        scratch_shapes=[
            buf(*features.shape),
            buf(own_nodes, width),
            buf(NB, BLK, dtype=jnp.int32),
            buf(*weights1.shape),
            buf(*weights2.shape),
            buf(NB, feat_part, BLK),
            buf(FEATS, OWN, hid_part, BLK),
            dma(2, 5, 4),
            dma(2, 5, 4),
            dma(4, FEATS - 1),
            dma(4, FEATS - 1),
            dma(6),
        ],
        compiler_params=limit(12, 1),
        name="gather_features",
    )(features, weights1, weights2, cotangent, degree_rows)

    held = buf(STAGES, BATCH, GROUP, BLK, BLK)
    listed = pltpu.SMEM((NB * 4 + 2 * BATCH,), jnp.int32)
    slot_cols = tile_cols.T
    feat_mean, back_parts = pl.pallas_call(
        both_kernel,
        out_shape=(shape(NB, feat_part, BLK), shape(block_total, hid_part, BLK)),
        in_specs=[SMEM, SMEM, ANY, VMEM, VMEM, VMEM],
        out_specs=(VMEM, VMEM),
        scratch_shapes=[
            held,
            buf(NB, feat_part, BLK, dtype=F32),
            buf(block_total, hid_part, BLK, dtype=F32),
            listed,
            dma(STAGES, BATCH),
        ],
        compiler_params=limit(36),
        name="aggregate_both",
    )(
        slot_cols,
        tile_counts,
        groups,
        all_feats.reshape(block_total, feat_part, BLK),
        spread.reshape(NB, hid_part, BLK),
        degree_rows,
    )

    row = (SIDE, HALF, hid_part, BLK)
    part_row = (SIDE, QUARTER, hid_part, BLK)
    middle_bufs = (
        buf(2, 2, *part_row),
        buf(2, 2, *row),
        buf(2, 2, *part_row),
        buf(2, *row),
        buf(2, 2, *part_row[1:]),
        buf(2, 2, *row[1:]),
        buf(2, 2, *part_row[1:]),
    )
    first_rows, second_rows = 2 * feat_part, 2 * hid_part
    all_hidden, hidden, own_hidden, all_cotangent, first_part = pl.pallas_call(
        middle_kernel,
        out_shape=(
            shape(shard_total, NB, hid_part, BLK),
            shape(FEATS, OWN, hid_part, BLK),
            shape(NB, hid_part, BLK),
            shape(FEATS, own_nodes, width),
            shape(first_rows // 8 * 2, 8, BLK, dtype=F32),
        ),
        in_specs=[VMEM] * 6 + [HBM],
        out_specs=(ANY, VMEM, VMEM, ANY, VMEM),
        scratch_shapes=[
            buf(own_nodes, width),
            buf(FEATS, OWN, feat_part, BLK),
            buf(OWN, width, BLK),
            buf(NB, hid_part, BLK),
            buf(FEATS, OWN, hid_part, BLK),
            buf(FEATS, first_rows, width, dtype=F32),
            buf(FEATS, first_rows, width, dtype=F32),
            middle_bufs,
            dma(2, 5, 4),
            dma(2, 5, 4),
            dma(2, 2, 2, 3),
            dma(2, 2, 2, 3),
            dma(5, FEATS - 1),
            dma(5, FEATS - 1),
            dma(3),
        ],
        compiler_params=limit(24, 2),
        name="first_layer",
    )(
        feat_mean,
        back_parts.reshape(SIDE, SIDE, NB, hid_part, BLK),
        own_feats,
        all_weights1,
        bias1.reshape(1, width),
        all_weights2,
        cotangent,
    )

    hidden_mean, second_part = pl.pallas_call(
        mean_kernel,
        out_shape=(shape(NB, hid_part, BLK), shape(second_rows // 8 * 2, 8, BLK, dtype=F32)),
        in_specs=[SMEM, SMEM, ANY, VMEM, VMEM, VMEM, VMEM],
        out_specs=(VMEM, VMEM),
        scratch_shapes=[held, buf(NB, hid_part, BLK, dtype=F32), listed, dma(STAGES, BATCH)],
        compiler_params=limit(24),
        name="aggregate_hidden",
    )(
        slot_cols,
        tile_counts,
        groups,
        all_hidden.reshape(block_total, hid_part, BLK),
        degree_rows,
        own_hidden,
        all_cotangent.reshape(NB, BLK, width),
    )

    pieces = (shard_total, 2, 8, BLK)
    means, summed = pl.pallas_call(
        last_kernel,
        out_shape=(shape(FEATS, OWN, hid_part, BLK), shape(*pieces, dtype=F32)),
        in_specs=[VMEM] * 3,
        out_specs=(VMEM, VMEM),
        scratch_shapes=[
            buf(*pieces, dtype=F32),
            buf(*pieces, dtype=F32),
            dma(FEATS - 1),
            dma(FEATS - 1),
            dma(2, shard_total - 1),
            dma(2, shard_total - 1),
        ],
        compiler_params=limit(8, 3),
        name="regroup_mean",
    )(hidden_mean, first_part, second_part)
    hidden_out, grad_second, grad_first = pl.pallas_call(
        functools.partial(out_kernel, scale),
        out_shape=(
            shape(own_nodes, width),
            shape(second_rows, width, dtype=F32),
            shape(first_rows, width, dtype=F32),
        ),
        in_specs=[VMEM] * 5,
        out_specs=(VMEM, VMEM, VMEM),
        compiler_params=limit(8),
        name="second_layer",
    )(hidden, means, all_weights2, bias2.reshape(1, width), summed)
    return (
        hidden_out,
        grad_second.reshape(2, hid_part, width),
        grad_first.reshape(2, feat_part, width),
    )


def solution(mesh):
    return jax.shard_map(
        shards,
        mesh=mesh,
        in_specs=(
            P("feat", "node"),
            P("node", None),
            P("node"),
            P("node", None, None, None),
            P("node"),
            P(None, "feat", None),
            P(),
            P(None, "feat", None),
            P(),
            P(("node", "feat"), None),
        ),
        out_specs=(P(("node", "feat"), None), P(None, "feat", None), P(None, "feat", None)),
        check_vma=False,
    )
```

```python
import functools
import math

import jax
import jax.numpy as jnp
from jax import lax
from jax.experimental import pallas as pl
from jax.experimental.pallas import tpu as pltpu
from jax.sharding import PartitionSpec as P

MESH = pl.DeviceIdType.MESH
BF16 = jnp.bfloat16
F32 = jnp.float32
FEATS = 8
SIDE = 4
BLK = 128
NB = 48
OWN = NB // FEATS
HALF, QUARTER = NB // 2, NB // 4
GROUP = 4
BATCH = 8
STAGES = 4
ROW_STAGES = 3
AHEAD = (0, -1, 1, 2)
VMEM = pl.BlockSpec(memory_space=pltpu.VMEM)
SMEM = pl.BlockSpec(memory_space=pltpu.SMEM)
ANY = pl.BlockSpec(memory_space=pl.ANY)
HBM = pl.BlockSpec(memory_space=pltpu.HBM)


def dot(left, right, dims):
    return lax.dot_general(left, right, (dims, ((), ())), preferred_element_type=F32)


class Place:
    def __init__(self):
        self.feat = lax.axis_index("feat")
        self.node = lax.axis_index("node")
        self.x = self.node // SIDE
        self.z = self.node % SIDE

    def peer(self, step):
        return (self.feat + step + FEATS) % FEATS

    def shift(self, dx, dz):
        return ((self.x + dx + SIDE) % SIDE) * SIDE + (self.z + dz + SIDE) % SIDE

    def beside(self):
        return [self.shift(dx, dz) for dx, dz in ((1, 0), (-1, 0), (0, 1), (0, -1))]

    def others(self):
        total = SIDE * SIDE
        return [(self.node + step) % total for step in range(1, total)]

    def turned(self, half, first, second):
        return self.shift(first, second) if half == 0 else self.shift(second, first)

    def greet(self, nodes):
        barrier = pltpu.get_barrier_semaphore()
        others = [{"feat": self.peer(step)} for step in range(1, FEATS)]
        others += [{"node": node} for node in nodes]
        for other in others:
            pl.semaphore_signal(barrier, inc=1, device_id=other, device_id_type=MESH)
        pl.semaphore_wait(barrier, len(others))


class Copies:
    def __init__(self):
        self.sent = []

    def send(self, source, target, send_sem, recv_sem, device):
        copy = pltpu.make_async_remote_copy(
            src_ref=source,
            dst_ref=target,
            send_sem=send_sem,
            recv_sem=recv_sem,
            device_id=device,
            device_id_type=MESH,
        )
        copy.start()
        self.sent.append(copy)
        return copy

    def finish(self):
        for copy in self.sent:
            copy.wait_send()


class Regroup:
    def __init__(self, copies, place, source_at, target_at, send_sems, recv_sems):
        self.parts = []
        for step in range(1, FEATS):
            to = place.peer(step)
            self.parts.append(
                copies.send(
                    source_at(to),
                    target_at(place.feat),
                    send_sems.at[step - 1],
                    recv_sems.at[step - 1],
                    {"feat": to},
                )
            )
        target_at(place.feat)[...] = source_at(place.feat)[...]

    def wait(self):
        for part in self.parts:
            part.wait_recv()


class Broadcast:
    def __init__(self, copies, place, source, target, send_sems, recv_sems):
        self.copies, self.place, self.target = copies, place, target
        self.send_sems, self.recv_sems = send_sems, recv_sems
        self.other = place.feat + 1 - 2 * (place.feat % 2)
        slot = target.at[place.feat]
        self.parts = [self._send(step - 1, source, slot, place.peer(2 * step)) for step in range(1, SIDE)]
        self.parts.append(self._send(SIDE - 1, source, slot, self.other))

    def _send(self, number, source, target, to):
        return self.copies.send(
            source, target, self.send_sems.at[number], self.recv_sems.at[number], {"feat": to}
        )

    def forward(self):
        for step in range(1, SIDE):
            self.parts[step - 1].wait_recv()
            slot = self.target.at[self.place.peer(-2 * step)]
            self.parts.append(self._send(SIDE - 1 + step, slot, slot, self.other))

    def wait(self):
        for part in self.parts[SIDE - 1 :]:
            part.wait_recv()


class Gather:
    def __init__(self, copies, place, own, out, send_sems, recv_sems):
        self.copies, self.place, self.own, self.out = copies, place, own, out
        self.send_sems, self.recv_sems = send_sems, recv_sems
        self.made = {}

    def _send(self, half, unit, role, source, target, first, second):
        place = self.place
        self.made[half, unit, role] = self.copies.send(
            source,
            target,
            self.send_sems.at[half, unit, role],
            self.recv_sems.at[half, unit, role],
            {"node": place.turned(half, first, second)},
        )

    def full(self, half, unit):
        rows = pl.ds(half * HALF, HALF)
        ahead = 0 if unit == SIDE else AHEAD[unit]
        shard = self.place.turned(half, ahead, 0)
        source = self.own.at[rows] if ahead == 0 else self.out.at[shard, rows]
        for role, way in ((0, 1), (1, -1)):
            move = (way, 0) if unit == SIDE else (0, way)
            self._send(half, unit, role, source, self.out.at[shard, rows], *move)

    def forward(self, half, unit, role):
        way = 1 if role == 0 else -1
        self.made[half, unit, role].wait_recv()
        rows = pl.ds(half * HALF + role * QUARTER, QUARTER)
        if unit == SIDE:
            shard, move = self.place.turned(half, -way, 0), (way, 0)
        else:
            shard, move = self.place.turned(half, AHEAD[unit], -way), (0, way)
        part = self.out.at[shard, rows]
        self._send(half, unit, role + 2, part, part, *move)

    def arrived(self, half, unit):
        for role in (2, 3):
            self.made[half, unit, role].wait_recv()

    def start(self):
        for half in range(2):
            self.full(half, SIDE)

    def start_columns(self):
        for half in range(2):
            self.full(half, 0)

    def rows(self):
        for role in range(2):
            for half in range(2):
                self.forward(half, SIDE, role)
                self.full(half, role + 1)

    def near(self):
        for role in range(2):
            for half in range(2):
                self.forward(half, 0, role)
        for half in range(2):
            self.arrived(half, SIDE)
            self.full(half, 3)

    def far(self, units=(1, 2, 3)):
        for unit in units:
            for role in range(2):
                for half in range(2):
                    self.forward(half, unit, role)

    def last(self):
        for unit in range(SIDE):
            for half in range(2):
                self.arrived(half, unit)


class Scatter:
    def __init__(self, copies, place, parts, bufs, send_sems, recv_sems):
        self.copies, self.place, self.parts = copies, place, parts
        self.pass1, self.got1, self.sum1, self.half1, self.pass2, self.got2, self.sum2 = bufs
        self.send_sems, self.recv_sems = send_sems, recv_sems
        self.made = {}

    def _send(self, half, phase, side, kind, source, target):
        way = 1 if side == 0 else -1
        first, second = (way, 0) if phase == 0 else (0, way)
        self.made[half, phase, side, kind] = self.copies.send(
            source,
            target,
            self.send_sems.at[half, phase, side, kind],
            self.recv_sems.at[half, phase, side, kind],
            {"node": self.place.turned(half, first, second)},
        )

    def _line(self, half, ahead, quarter=None):
        rows = pl.ds(half * HALF, HALF)
        if quarter is not None:
            rows = pl.ds(half * HALF + quarter * QUARTER, QUARTER)
        if half == 0:
            return self.parts.at[(self.place.x + ahead + SIDE) % SIDE, :, rows]
        return self.parts.at[:, (self.place.z + ahead + SIDE) % SIDE, rows]

    def _unit(self, half, ahead, quarter):
        at = self.place.z if half == 0 else self.place.x
        rows = pl.ds(quarter * QUARTER, QUARTER)
        return self.half1.at[half, (at + ahead + SIDE) % SIDE, rows]

    def start(self):
        for half in range(2):
            for side, way in ((0, 1), (1, -1)):
                self._send(half, 0, side, 0, self._line(half, 2 * way, side), self.pass1.at[half, side])

    def direct(self):
        for half in range(2):
            for side, way in ((0, 1), (1, -1)):
                rows = pl.ds((1 - side) * QUARTER, QUARTER)
                self._send(half, 0, side, 1, self._line(half, way, 1 - side), self.got1.at[half, side, :, rows])

    def middle(self):
        for side, way in ((0, 1), (1, -1)):
            for half in range(2):
                self.made[half, 0, side, 0].wait_recv()
                mine, came, total = self._line(half, way, side), self.pass1.at[half, side], self.sum1.at[half, side]

                @pl.loop(0, SIDE)
                def _(shard):
                    total[shard] = (mine[shard].astype(F32) + came[shard].astype(F32)).astype(BF16)

                rows = pl.ds(side * QUARTER, QUARTER)
                self._send(half, 0, side, 2, total, self.got1.at[half, side, :, rows])

    def turn(self):
        for half in range(2):
            for side in range(2):
                for kind in (1, 2):
                    self.made[half, 0, side, kind].wait_recv()
            mine, left, right, total = self._line(half, 0), self.got1.at[half, 0], self.got1.at[half, 1], self.half1.at[half]

            @pl.loop(0, SIDE)
            def _(shard):
                near = left[shard].astype(F32) + right[shard].astype(F32)
                total[shard] = (mine[shard].astype(F32) + near).astype(BF16)

            for side, way in ((0, 1), (1, -1)):
                self._send(half, 1, side, 0, self._unit(half, 2 * way, side), self.pass2.at[half, side])
            for side, way in ((0, 1), (1, -1)):
                rows = pl.ds((1 - side) * QUARTER, QUARTER)
                self._send(half, 1, side, 1, self._unit(half, way, 1 - side), self.got2.at[half, side, rows])

    def middle2(self):
        for side, way in ((0, 1), (1, -1)):
            for half in range(2):
                self.made[half, 1, side, 0].wait_recv()
                total = self.sum2.at[half, side]
                mine, came = self._unit(half, way, side)[...], self.pass2[half, side]
                total[...] = (mine.astype(F32) + came.astype(F32)).astype(BF16)
                rows = pl.ds(side * QUARTER, QUARTER)
                self._send(half, 1, side, 2, total, self.got2.at[half, side, rows])

    def end(self, out):
        for half in range(2):
            for side in range(2):
                for kind in (1, 2):
                    self.made[half, 1, side, kind].wait_recv()
            for quarter in range(2):
                rows = pl.ds(quarter * QUARTER, QUARTER)
                near = self.got2[half, 0, rows].astype(F32) + self.got2[half, 1, rows].astype(F32)
                total = self._unit(half, 0, quarter)[...].astype(F32) + near
                out[pl.ds(half * HALF + quarter * QUARTER, QUARTER)] = total.astype(BF16)


class Total:
    def __init__(self, copies, place, part, came, summed, send_sems, recv_sems):
        self.copies, self.place, self.part, self.came, self.summed = copies, place, part, came, summed
        self.send_sems, self.recv_sems = send_sems, recv_sems

    def _all(self, phase, source_at, target):
        place = self.place
        self.parts = []
        for number, node in enumerate(place.others()):
            self.parts.append(
                self.copies.send(
                    source_at(node),
                    target.at[place.node],
                    self.send_sems.at[phase, number],
                    self.recv_sems.at[phase, number],
                    {"node": node},
                )
            )

    def start(self):
        self._all(0, lambda node: self.part.at[node], self.came)
        self.came[self.place.node] = self.part[self.place.node]

    def turn(self):
        for part in self.parts:
            part.wait_recv()
        self.summed[self.place.node] = sum(self.came[slot] for slot in range(SIDE * SIDE))
        self._all(1, lambda node: self.summed.at[self.place.node], self.summed)

    def end(self):
        for part in self.parts:
            part.wait_recv()


def own_rows(feat):
    return pl.ds(feat * OWN, OWN)


def gather_kernel(
    features_in, weights1, weights2, cotangent_in, degrees_in,
    all_feats, own_feats, all_weights1, all_weights2, spread,
    features, cotangent, degrees, own_weights1, own_weights2, blocks, outgoing,
    gather_send, gather_recv, feat_send, feat_recv, local_sems,
):
    place, copies = Place(), Copies()
    pairs = (
        (features_in, features),
        (weights2, own_weights2),
        (weights1, own_weights1),
        (cotangent_in, cotangent),
        (degrees_in, degrees),
    )
    loads = [pltpu.make_async_copy(pair[0], pair[1], local_sems.at[number]) for number, pair in enumerate(pairs)]
    for load in loads:
        load.start()
    place.greet(place.beside())
    loads[0].wait()
    for block in range(NB):
        blocks[block] = features[:, block * BLK : (block + 1) * BLK]
    gather = Gather(copies, place, blocks, all_feats, gather_send, gather_recv)
    gather.start()
    gather.start_columns()
    regroups = []
    for number, (weights, target) in enumerate(((own_weights2, all_weights2), (own_weights1, all_weights1))):
        loads[1 + number].wait()
        regroups.append(
            Regroup(
                copies, place, lambda to: weights, lambda slot: target.at[slot], feat_send.at[number], feat_recv.at[number]
            )
        )
    own = pltpu.make_async_copy(blocks, all_feats.at[place.node], local_sems.at[len(pairs)])
    own.start()
    gather.rows()
    loads[3].wait()
    loads[4].wait()
    regroups[0].wait()
    neighbour = all_weights2[:, 1].reshape(-1, all_weights2.shape[-1])
    for block in range(OWN):
        nodes = cotangent[block * BLK : (block + 1) * BLK, :]
        back = dot(neighbour, nodes, ((1,), (1,)))
        degree = degrees[pl.ds(place.feat * OWN + block, 1), :].astype(F32)
        outgoing[:, block] = (back / degree).astype(BF16).reshape(FEATS, -1, BLK)
    regroups.append(
        Regroup(
            copies, place, lambda to: outgoing.at[to], lambda slot: spread.at[slot], feat_send.at[3], feat_recv.at[3]
        )
    )
    gather.near()
    regroups.append(
        Regroup(
            copies, place, lambda to: blocks.at[own_rows(to)], lambda slot: own_feats.at[slot], feat_send.at[2], feat_recv.at[2]
        )
    )
    gather.far()
    for regroup in regroups[1:]:
        regroup.wait()
    gather.last()
    own.wait()
    copies.finish()


def plan_groups(counts, groups):
    def row(block, total):
        for part in range(4):
            groups[total + part] = block * 4 + part
        return total + (counts[block] + GROUP - 1) // GROUP

    total = lax.fori_loop(0, NB, row, jnp.int32(0))
    for part in range(BATCH):
        groups[total + part] = 0
    return total


def each_step(counts, groups, tiles, held, tile_sems, clear, work):
    total = plan_groups(counts, groups)
    steps = (total + BATCH - 1) // BATCH

    def fetch(step):
        @pl.when(step < steps)
        def _():
            slot = step % STAGES
            for place in range(BATCH):
                group = groups[step * BATCH + place]
                pltpu.make_async_copy(tiles.at[group], held.at[slot, place], tile_sems.at[slot]).start()

    for step in range(STAGES - 1):
        fetch(step)
    clear()

    def body(step, carry):
        fetch(step + STAGES - 1)
        slot = step % STAGES
        pltpu.make_async_copy(tiles.at[pl.ds(0, BATCH)], held.at[slot], tile_sems.at[slot]).wait()
        entries = []
        for place in range(BATCH):
            group = groups[step * BATCH + place]
            block, first = group // 4, (group % 4) * GROUP
            live = jnp.where(step * BATCH + place < total, counts[block], 0)
            wide = jnp.concatenate([held[slot, place, part] for part in range(GROUP)], axis=1)
            entries.append((block, first, live, wide))
        work(entries)
        return carry

    lax.fori_loop(0, steps, body, jnp.int32(0))


def picked(source, cols, entry):
    block, first, live, wide = entry
    parts = []
    for slot in range(GROUP):
        value = source[cols[first + slot, block]]
        parts.append(jnp.where(first + slot < live, value, jnp.zeros_like(value)))
    return dot(jnp.concatenate(parts, axis=1), wide, ((1,), (1,)))


def load_all(pairs, sems):
    loads = [pltpu.make_async_copy(pair[0], pair[1], sems.at[number]) for number, pair in enumerate(pairs)]
    for load in loads:
        load.start()
    for load in loads:
        load.wait()


def back_kernel(cols_in, counts_in, tiles, spread, back, cols, counts, held, sums, groups, tile_sems, load_sems):
    load_all(((cols_in, cols), (counts_in, counts)), load_sems)

    def clear():
        @pl.loop(0, sums.shape[0] // 16)
        def _(part):
            sums[pl.ds(part * 16, 16)] = jnp.zeros((16,) + sums.shape[1:], F32)

    def work(entries):
        backs = [dot(spread[entry[0]], entry[3], ((1,), (0,))) for entry in entries]
        for (block, first, live, _), product in zip(entries, backs):
            for slot in range(GROUP):
                part = product[:, slot * BLK : (slot + 1) * BLK]
                sums[cols[first + slot, block]] += jnp.where(first + slot < live, part, jnp.zeros_like(part))

    each_step(counts, groups, tiles, held, tile_sems, clear, work)

    @pl.loop(0, sums.shape[0] // 16)
    def _(part):
        rows = pl.ds(part * 16, 16)
        back[rows] = sums[rows].astype(BF16)


def mean_kernel(
    cols_in, counts_in, tiles, source, degrees_in, hidden, cotangent,
    mean, grads,
    cols, counts, degrees, held, sums, groups, tile_sems, load_sems,
):
    load_all(((cols_in, cols), (counts_in, counts), (degrees_in, degrees)), load_sems)

    def clear():
        sums[...] = jnp.zeros_like(sums)

    def work(entries):
        products = [picked(source, cols, entry) for entry in entries]
        for entry, product in zip(entries, products):
            sums[entry[0]] += product

    each_step(counts, groups, tiles, held, tile_sems, clear, work)

    @pl.loop(0, NB)
    def _(block):
        mean[block] = (sums[block] / degrees[pl.ds(block, 1), :].astype(F32)).astype(BF16)

    wide = 8
    total = jnp.zeros((2 * hidden.shape[1], cotangent.shape[-1]), F32)

    def add(part, total):
        blocks = [part * wide + block for block in range(wide)]
        stack = [jnp.concatenate([hidden[block], mean[block]], axis=0) for block in blocks]
        nodes = cotangent[pl.ds(part * wide, wide)].reshape(wide * BLK, -1)
        return total + dot(jnp.concatenate(stack, axis=1), nodes, ((1,), (0,)))

    put_tiles(grads, lax.fori_loop(0, NB // wide, add, total))


def put_tiles(out, value):
    for tile in range(out.shape[0]):
        out[tile] = value[tile // 2 * 8 : tile // 2 * 8 + 8, tile % 2 * BLK : tile % 2 * BLK + BLK]


def middle_kernel(
    cols, counts, tiles, all_feats, degrees, back_parts, own_feats, weights1, bias1, weights2, cotangent_in,
    all_hidden, hidden, own_hidden, all_cotangent, grad_first,
    held, cotangent, feat_mean, means, slopes, back, own_back, grads, feat_buf, bufs,
    gather_send, gather_recv, scatter_send, scatter_recv, feat_send, feat_recv, tile_sems, local_sems,
):
    place, copies = Place(), Copies()

    def tile_copy(step):
        slot = step % ROW_STAGES
        return pltpu.make_async_copy(tiles.at[own_rows(place.peer(step + 1))], held.at[slot], tile_sems.at[slot])

    for step in range(ROW_STAGES - 1):
        tile_copy(step).start()
    load = pltpu.make_async_copy(cotangent_in, cotangent, local_sems.at[0])
    load.start()
    place.greet(place.beside())

    def regroup(number, source_at, target_at):
        return Regroup(copies, place, source_at, target_at, feat_send.at[number], feat_recv.at[number])

    def mean_copy(step):
        to = place.peer(step + 1)
        return pltpu.make_async_remote_copy(
            src_ref=feat_mean.at[own_rows(to)],
            dst_ref=means.at[place.feat],
            send_sem=feat_send.at[0, step],
            recv_sem=feat_recv.at[0, step],
            device_id={"feat": to},
            device_id_type=MESH,
        )

    def own_blocks(step):
        tile_copy(step).wait()
        for part in range(OWN):
            block = place.peer(step + 1) * OWN + part
            parts = []
            for slot in range(tiles.shape[1]):
                value = all_feats[cols[slot, block]]
                parts.append(jnp.where(slot < counts[block], value, jnp.zeros_like(value)))
            wide = jnp.concatenate([held[step % ROW_STAGES, part, slot] for slot in range(tiles.shape[1])], axis=1)
            total = dot(jnp.concatenate(parts, axis=1), wide, ((1,), (1,)))
            feat_mean[block] = (total / degrees[pl.ds(block, 1), :].astype(F32)).astype(BF16)

    def send_blocks(step, carry):
        @pl.when(step + ROW_STAGES - 1 < FEATS)
        def _():
            tile_copy(step + ROW_STAGES - 1).start()

        own_blocks(step)
        mean_copy(step).start()
        return carry

    scatter = Scatter(copies, place, back_parts, bufs, scatter_send, scatter_recv)
    scatter.start()
    first = weights1[...].reshape(-1, weights1.shape[-1])
    bias = jnp.transpose(jnp.broadcast_to(bias1[...], (BLK, bias1.shape[1])))
    lax.fori_loop(0, 3, send_blocks, jnp.int32(0))
    scatter.direct()
    lax.fori_loop(3, FEATS - 1, send_blocks, jnp.int32(0))
    own_blocks(FEATS - 1)
    means[place.feat] = feat_mean[own_rows(place.feat)]
    for step in range(FEATS - 1):
        mean_copy(step).wait()

    def stack(block):
        parts = []
        for part in range(FEATS):
            parts += [own_feats[part, block], means[part, block]]
        return jnp.concatenate(parts, axis=0)

    for block in range(OWN):
        pre = dot(first, stack(block), ((0,), (0,))) + bias
        sigmoid = jax.nn.sigmoid(pre)
        slopes[block] = (sigmoid * (1.0 + pre * (1.0 - sigmoid))).astype(BF16)
        hidden[:, block] = (pre * sigmoid).astype(BF16).reshape(FEATS, -1, BLK)
    to_hidden = regroup(1, lambda to: hidden.at[to], lambda slot: own_hidden.at[own_rows(slot)])
    scatter.middle()
    to_hidden.wait()
    gather = Gather(copies, place, own_hidden, all_hidden, gather_send, gather_recv)
    gather.start()
    own = pltpu.make_async_copy(own_hidden, all_hidden.at[place.node], local_sems.at[1])
    own.start()
    load.wait()
    to_cotangent = Broadcast(copies, place, cotangent, all_cotangent, feat_send.at[4], feat_recv.at[4])
    own_cotangent = pltpu.make_async_copy(cotangent, all_cotangent.at[place.feat], local_sems.at[2])
    own_cotangent.start()
    scatter.turn()
    gather.start_columns()
    gather.rows()
    scatter.middle2()
    gather.near()
    scatter.end(back)
    to_back = regroup(2, lambda to: back.at[own_rows(to)], lambda slot: own_back.at[slot])
    gather.far((1, 2))
    to_back.wait()
    own_weights = weights2[:, 0].reshape(-1, weights2.shape[-1])
    total = None
    for block in range(OWN):
        nodes = cotangent[block * BLK : (block + 1) * BLK, :]
        came = jnp.concatenate([own_back[part, block] for part in range(FEATS)], axis=0)
        grad = dot(own_weights, nodes, ((1,), (1,))) + came.astype(F32)
        grad = (grad * slopes[block].astype(F32)).astype(BF16)
        product = dot(stack(block), grad, ((1,), (1,)))
        total = product if total is None else total + product
    grads[...] = total.reshape(grads.shape)
    to_total = regroup(3, lambda to: grads.at[to], lambda slot: feat_buf.at[slot])
    gather.far((3,))
    to_cotangent.forward()
    to_total.wait()
    put_tiles(grad_first, sum(feat_buf[slot] for slot in range(FEATS)))
    gather.last()
    to_cotangent.wait()
    own_cotangent.wait()
    own.wait()
    copies.finish()


def last_kernel(
    hidden_mean, grad_first, grad_second,
    means, summed,
    part, came, feat_send, feat_recv, total_send, total_recv,
):
    place, copies = Place(), Copies()
    place.greet(place.others())
    to_means = Regroup(
        copies, place, lambda to: hidden_mean.at[own_rows(to)], lambda slot: means.at[slot], feat_send, feat_recv
    )
    part[:, 1] = jnp.zeros_like(part[:, 1])
    part[:, 0] = grad_second[...]
    part[pl.ds(0, grad_first.shape[0]), 1] = grad_first[...]
    total = Total(copies, place, part, came, summed, total_send, total_recv)
    total.start()
    total.turn()
    total.end()
    to_means.wait()
    copies.finish()


def out_kernel(scale, hidden, means, weights2, bias2, summed, hidden_out, grad_second, grad_first):
    second = weights2[...].reshape(-1, weights2.shape[-1])
    for block in range(OWN):
        parts = []
        for part in range(FEATS):
            parts += [hidden[part, block], means[part, block]]
        out = dot(jnp.concatenate(parts, axis=0), second, ((0,), (0,))) + bias2[...]
        hidden_out[block * BLK : (block + 1) * BLK, :] = out.astype(BF16)
    for kind, grad in enumerate((grad_second, grad_first)):
        for tile in range(grad.shape[0] // 8 * 2):
            rows, columns = pl.ds(tile // 2 * 8, 8), pl.ds(tile % 2 * BLK, BLK)
            grad[rows, columns] = summed[tile, kind] * scale


def limit(mib, collective_id=None):
    if collective_id is None:
        return pltpu.CompilerParams(vmem_limit_bytes=mib * 1024 * 1024)
    return pltpu.CompilerParams(
        collective_id=collective_id, has_side_effects=True, vmem_limit_bytes=mib * 1024 * 1024
    )


def shape(*dims, dtype=BF16):
    return jax.ShapeDtypeStruct(dims, dtype)


def buf(*dims, dtype=BF16):
    return pltpu.VMEM(dims, dtype)


def dma(*dims):
    return pltpu.SemaphoreType.DMA(dims)


def in_hbm(array):
    return pltpu.with_memory_space_constraint(array, pltpu.HBM)


def shards(
    features, tile_cols, tile_counts, tiles, degrees, weights1, bias1, weights2, bias2, cotangent
):
    feat_part = features.shape[0]
    hid_part = weights2.shape[1]
    width = weights2.shape[2]
    shard_total = lax.axis_size("node")
    block_total = shard_total * NB
    scale = 1.0 / math.sqrt(features.shape[1] * shard_total)
    own_nodes = OWN * BLK
    degree_rows = degrees.reshape(NB, BLK)
    groups = tiles.reshape(NB * tiles.shape[1] // GROUP, GROUP, BLK, BLK)

    all_feats, own_feats, all_weights1, all_weights2, spread = pl.pallas_call(
        gather_kernel,
        out_shape=(
            shape(shard_total, NB, feat_part, BLK),
            shape(FEATS, OWN, feat_part, BLK),
            shape(FEATS, 2, feat_part, width),
            shape(FEATS, 2, hid_part, width),
            shape(FEATS, OWN, hid_part, BLK),
        ),
        in_specs=[HBM] * 5,
        out_specs=(ANY, VMEM, VMEM, VMEM, VMEM),
        scratch_shapes=[
            buf(*features.shape),
            buf(own_nodes, width),
            buf(NB, BLK, dtype=jnp.int32),
            buf(*weights1.shape),
            buf(*weights2.shape),
            buf(NB, feat_part, BLK),
            buf(FEATS, OWN, hid_part, BLK),
            dma(2, 5, 4),
            dma(2, 5, 4),
            dma(4, FEATS - 1),
            dma(4, FEATS - 1),
            dma(6),
        ],
        compiler_params=limit(12, 1),
        name="gather_features",
    )(*[in_hbm(array) for array in (features, weights1, weights2, cotangent, degree_rows)])

    held = buf(STAGES, BATCH, GROUP, BLK, BLK)
    planned = pltpu.SMEM((NB * 4 + 2 * BATCH,), jnp.int32)
    slot_cols = tile_cols.T
    listed = [pltpu.SMEM((tiles.shape[1], NB), jnp.int32), pltpu.SMEM((NB,), jnp.int32)]
    back_parts = pl.pallas_call(
        back_kernel,
        out_shape=shape(block_total, hid_part, BLK),
        in_specs=[HBM, HBM, ANY, VMEM],
        out_specs=VMEM,
        scratch_shapes=[
            *listed,
            held,
            buf(block_total, hid_part, BLK, dtype=F32),
            planned,
            dma(STAGES),
            dma(2),
        ],
        compiler_params=limit(28),
        name="aggregate_back",
    )(in_hbm(slot_cols), in_hbm(tile_counts), groups, spread.reshape(NB, hid_part, BLK))

    row = (SIDE, HALF, hid_part, BLK)
    part_row = (SIDE, QUARTER, hid_part, BLK)
    middle_bufs = (
        buf(2, 2, *part_row),
        buf(2, 2, *row),
        buf(2, 2, *part_row),
        buf(2, *row),
        buf(2, 2, *part_row[1:]),
        buf(2, 2, *row[1:]),
        buf(2, 2, *part_row[1:]),
    )
    first_rows, second_rows = 2 * feat_part, 2 * hid_part
    all_hidden, hidden, own_hidden, all_cotangent, first_part = pl.pallas_call(
        middle_kernel,
        out_shape=(
            shape(shard_total, NB, hid_part, BLK),
            shape(FEATS, OWN, hid_part, BLK),
            shape(NB, hid_part, BLK),
            shape(FEATS, own_nodes, width),
            shape(first_rows // 8 * 2, 8, BLK, dtype=F32),
        ),
        in_specs=[SMEM, SMEM, ANY] + [VMEM] * 7 + [HBM],
        out_specs=(ANY, VMEM, VMEM, ANY, VMEM),
        scratch_shapes=[
            buf(ROW_STAGES, OWN, *tiles.shape[1:]),
            buf(own_nodes, width),
            buf(NB, feat_part, BLK),
            buf(FEATS, OWN, feat_part, BLK),
            buf(OWN, width, BLK),
            buf(NB, hid_part, BLK),
            buf(FEATS, OWN, hid_part, BLK),
            buf(FEATS, first_rows, width, dtype=F32),
            buf(FEATS, first_rows, width, dtype=F32),
            middle_bufs,
            dma(2, 5, 4),
            dma(2, 5, 4),
            dma(2, 2, 2, 3),
            dma(2, 2, 2, 3),
            dma(5, FEATS - 1),
            dma(5, FEATS - 1),
            dma(ROW_STAGES),
            dma(3),
        ],
        compiler_params=limit(32, 2),
        name="first_layer",
    )(
        slot_cols,
        tile_counts,
        tiles,
        all_feats.reshape(block_total, feat_part, BLK),
        degree_rows,
        back_parts.reshape(SIDE, SIDE, NB, hid_part, BLK),
        own_feats,
        all_weights1,
        bias1.reshape(1, width),
        all_weights2,
        in_hbm(cotangent),
    )

    hidden_mean, second_part = pl.pallas_call(
        mean_kernel,
        out_shape=(shape(NB, hid_part, BLK), shape(second_rows // 8 * 2, 8, BLK, dtype=F32)),
        in_specs=[HBM, HBM, ANY, VMEM, HBM, VMEM, VMEM],
        out_specs=(VMEM, VMEM),
        scratch_shapes=[
            *listed,
            buf(NB, BLK, dtype=jnp.int32),
            held,
            buf(NB, hid_part, BLK, dtype=F32),
            planned,
            dma(STAGES),
            dma(3),
        ],
        compiler_params=limit(24),
        name="aggregate_hidden",
    )(
        in_hbm(slot_cols),
        in_hbm(tile_counts),
        groups,
        all_hidden.reshape(block_total, hid_part, BLK),
        in_hbm(degree_rows),
        own_hidden,
        all_cotangent.reshape(NB, BLK, width),
    )

    pieces = (shard_total, 2, 8, BLK)
    means, summed = pl.pallas_call(
        last_kernel,
        out_shape=(shape(FEATS, OWN, hid_part, BLK), shape(*pieces, dtype=F32)),
        in_specs=[VMEM] * 3,
        out_specs=(VMEM, VMEM),
        scratch_shapes=[
            buf(*pieces, dtype=F32),
            buf(*pieces, dtype=F32),
            dma(FEATS - 1),
            dma(FEATS - 1),
            dma(2, shard_total - 1),
            dma(2, shard_total - 1),
        ],
        compiler_params=limit(8, 3),
        name="regroup_mean",
    )(hidden_mean, first_part, second_part)
    hidden_out, grad_second, grad_first = pl.pallas_call(
        functools.partial(out_kernel, scale),
        out_shape=(
            shape(own_nodes, width),
            shape(second_rows, width, dtype=F32),
            shape(first_rows, width, dtype=F32),
        ),
        in_specs=[VMEM] * 5,
        out_specs=(VMEM, VMEM, VMEM),
        compiler_params=limit(8),
        name="second_layer",
    )(hidden, means, all_weights2, bias2.reshape(1, width), summed)
    return (
        hidden_out,
        grad_second.reshape(2, hid_part, width),
        grad_first.reshape(2, feat_part, width),
    )


def solution(mesh):
    return jax.shard_map(
        shards,
        mesh=mesh,
        in_specs=(
            P("feat", "node"),
            P("node", None),
            P("node"),
            P("node", None, None, None),
            P("node"),
            P(None, "feat", None),
            P(),
            P(None, "feat", None),
            P(),
            P(("node", "feat"), None),
        ),
        out_specs=(P(("node", "feat"), None), P(None, "feat", None), P(None, "feat", None)),
        check_vma=False,
    )
```

```python
import functools
import math

import jax
import jax.numpy as jnp
from jax import lax
from jax.experimental import pallas as pl
from jax.experimental.pallas import tpu as pltpu
from jax.sharding import PartitionSpec as P

MESH = pl.DeviceIdType.MESH
BF16 = jnp.bfloat16
F32 = jnp.float32
FEATS = 8
SIDE = 4
BLK = 128
NB = 48
OWN = NB // FEATS
HALF, QUARTER = NB // 2, NB // 4
GROUP = 4
BATCH = 8
STAGES = 4
ROW_STAGES = 3
AHEAD = (0, -1, 1, 2)
VMEM = pl.BlockSpec(memory_space=pltpu.VMEM)
SMEM = pl.BlockSpec(memory_space=pltpu.SMEM)
ANY = pl.BlockSpec(memory_space=pl.ANY)
HBM = pl.BlockSpec(memory_space=pltpu.HBM)


def dot(left, right, dims):
    return lax.dot_general(left, right, (dims, ((), ())), preferred_element_type=F32)


class Place:
    def __init__(self):
        self.feat = lax.axis_index("feat")
        self.node = lax.axis_index("node")
        self.x = self.node // SIDE
        self.z = self.node % SIDE

    def peer(self, step):
        return (self.feat + step + FEATS) % FEATS

    def shift(self, dx, dz):
        return ((self.x + dx + SIDE) % SIDE) * SIDE + (self.z + dz + SIDE) % SIDE

    def beside(self):
        return [self.shift(dx, dz) for dx, dz in ((1, 0), (-1, 0), (0, 1), (0, -1))]

    def others(self):
        total = SIDE * SIDE
        return [(self.node + step) % total for step in range(1, total)]

    def turned(self, half, first, second):
        return self.shift(first, second) if half == 0 else self.shift(second, first)

    def greet(self, nodes):
        barrier = pltpu.get_barrier_semaphore()
        others = [{"feat": self.peer(step)} for step in range(1, FEATS)]
        others += [{"node": node} for node in nodes]
        for other in others:
            pl.semaphore_signal(barrier, inc=1, device_id=other, device_id_type=MESH)
        pl.semaphore_wait(barrier, len(others))


class Copies:
    def __init__(self):
        self.sent = []

    def send(self, source, target, send_sem, recv_sem, device):
        copy = pltpu.make_async_remote_copy(
            src_ref=source,
            dst_ref=target,
            send_sem=send_sem,
            recv_sem=recv_sem,
            device_id=device,
            device_id_type=MESH,
        )
        copy.start()
        self.sent.append(copy)
        return copy

    def finish(self):
        for copy in self.sent:
            copy.wait_send()


class Regroup:
    def __init__(self, copies, place, source_at, target_at, send_sems, recv_sems):
        self.parts = []
        for step in range(1, FEATS):
            to = place.peer(step)
            self.parts.append(
                copies.send(
                    source_at(to),
                    target_at(place.feat),
                    send_sems.at[step - 1],
                    recv_sems.at[step - 1],
                    {"feat": to},
                )
            )
        target_at(place.feat)[...] = source_at(place.feat)[...]

    def wait(self):
        for part in self.parts:
            part.wait_recv()


class Gather:
    def __init__(self, copies, place, own, out, send_sems, recv_sems):
        self.copies, self.place, self.own, self.out = copies, place, own, out
        self.send_sems, self.recv_sems = send_sems, recv_sems
        self.made = {}

    def _send(self, half, unit, role, source, target, first, second):
        place = self.place
        self.made[half, unit, role] = self.copies.send(
            source,
            target,
            self.send_sems.at[half, unit, role],
            self.recv_sems.at[half, unit, role],
            {"node": place.turned(half, first, second)},
        )

    def full(self, half, unit):
        rows = pl.ds(half * HALF, HALF)
        ahead = 0 if unit == SIDE else AHEAD[unit]
        shard = self.place.turned(half, ahead, 0)
        source = self.own.at[rows] if ahead == 0 else self.out.at[shard, rows]
        for role, way in ((0, 1), (1, -1)):
            move = (way, 0) if unit == SIDE else (0, way)
            self._send(half, unit, role, source, self.out.at[shard, rows], *move)

    def forward(self, half, unit, role):
        way = 1 if role == 0 else -1
        self.made[half, unit, role].wait_recv()
        rows = pl.ds(half * HALF + role * QUARTER, QUARTER)
        if unit == SIDE:
            shard, move = self.place.turned(half, -way, 0), (way, 0)
        else:
            shard, move = self.place.turned(half, AHEAD[unit], -way), (0, way)
        part = self.out.at[shard, rows]
        self._send(half, unit, role + 2, part, part, *move)

    def arrived(self, half, unit):
        for role in (2, 3):
            self.made[half, unit, role].wait_recv()

    def start(self):
        for half in range(2):
            self.full(half, SIDE)

    def start_columns(self):
        for half in range(2):
            self.full(half, 0)

    def rows(self):
        for role in range(2):
            for half in range(2):
                self.forward(half, SIDE, role)
                self.full(half, role + 1)

    def near(self):
        for role in range(2):
            for half in range(2):
                self.forward(half, 0, role)
        for half in range(2):
            self.arrived(half, SIDE)
            self.full(half, 3)

    def far(self, units=(1, 2, 3)):
        for unit in units:
            for role in range(2):
                for half in range(2):
                    self.forward(half, unit, role)

    def last(self):
        for unit in range(SIDE):
            for half in range(2):
                self.arrived(half, unit)


class Scatter:
    def __init__(self, copies, place, parts, bufs, send_sems, recv_sems):
        self.copies, self.place, self.parts = copies, place, parts
        self.pass1, self.got1, self.sum1, self.half1, self.pass2, self.got2, self.sum2 = bufs
        self.send_sems, self.recv_sems = send_sems, recv_sems
        self.made = {}

    def _send(self, half, phase, side, kind, source, target):
        way = 1 if side == 0 else -1
        first, second = (way, 0) if phase == 0 else (0, way)
        self.made[half, phase, side, kind] = self.copies.send(
            source,
            target,
            self.send_sems.at[half, phase, side, kind],
            self.recv_sems.at[half, phase, side, kind],
            {"node": self.place.turned(half, first, second)},
        )

    def _line(self, half, ahead, quarter=None):
        rows = pl.ds(half * HALF, HALF)
        if quarter is not None:
            rows = pl.ds(half * HALF + quarter * QUARTER, QUARTER)
        if half == 0:
            return self.parts.at[(self.place.x + ahead + SIDE) % SIDE, :, rows]
        return self.parts.at[:, (self.place.z + ahead + SIDE) % SIDE, rows]

    def _unit(self, half, ahead, quarter):
        at = self.place.z if half == 0 else self.place.x
        rows = pl.ds(quarter * QUARTER, QUARTER)
        return self.half1.at[half, (at + ahead + SIDE) % SIDE, rows]

    def start(self):
        for half in range(2):
            for side, way in ((0, 1), (1, -1)):
                self._send(half, 0, side, 0, self._line(half, 2 * way, side), self.pass1.at[half, side])

    def direct(self):
        for half in range(2):
            for side, way in ((0, 1), (1, -1)):
                rows = pl.ds((1 - side) * QUARTER, QUARTER)
                self._send(half, 0, side, 1, self._line(half, way, 1 - side), self.got1.at[half, side, :, rows])

    def middle(self):
        for side, way in ((0, 1), (1, -1)):
            for half in range(2):
                self.made[half, 0, side, 0].wait_recv()
                mine, came, total = self._line(half, way, side), self.pass1.at[half, side], self.sum1.at[half, side]

                @pl.loop(0, SIDE)
                def _(shard):
                    total[shard] = (mine[shard].astype(F32) + came[shard].astype(F32)).astype(BF16)

                rows = pl.ds(side * QUARTER, QUARTER)
                self._send(half, 0, side, 2, total, self.got1.at[half, side, :, rows])

    def lines_arrived(self):
        for half in range(2):
            for side in range(2):
                for kind in (1, 2):
                    self.made[half, 0, side, kind].wait_recv()

    def turn(self):
        for half in range(2):
            mine, left, right, total = self._line(half, 0), self.got1.at[half, 0], self.got1.at[half, 1], self.half1.at[half]

            @pl.loop(0, SIDE)
            def _(shard):
                near = left[shard].astype(F32) + right[shard].astype(F32)
                total[shard] = (mine[shard].astype(F32) + near).astype(BF16)

            for side, way in ((0, 1), (1, -1)):
                self._send(half, 1, side, 0, self._unit(half, 2 * way, side), self.pass2.at[half, side])
            for side, way in ((0, 1), (1, -1)):
                rows = pl.ds((1 - side) * QUARTER, QUARTER)
                self._send(half, 1, side, 1, self._unit(half, way, 1 - side), self.got2.at[half, side, rows])

    def middle2(self):
        for side, way in ((0, 1), (1, -1)):
            for half in range(2):
                self.made[half, 1, side, 0].wait_recv()
                total = self.sum2.at[half, side]
                mine, came = self._unit(half, way, side)[...], self.pass2[half, side]
                total[...] = (mine.astype(F32) + came.astype(F32)).astype(BF16)
                rows = pl.ds(side * QUARTER, QUARTER)
                self._send(half, 1, side, 2, total, self.got2.at[half, side, rows])

    def end(self, out):
        for half in range(2):
            for side in range(2):
                for kind in (1, 2):
                    self.made[half, 1, side, kind].wait_recv()
            for quarter in range(2):
                rows = pl.ds(quarter * QUARTER, QUARTER)
                near = self.got2[half, 0, rows].astype(F32) + self.got2[half, 1, rows].astype(F32)
                total = self._unit(half, 0, quarter)[...].astype(F32) + near
                out[pl.ds(half * HALF + quarter * QUARTER, QUARTER)] = total.astype(BF16)


class Exchange:
    def __init__(self, copies, place, source_at, target, send_sems, recv_sems):
        self.parts = []
        for number, node in enumerate(place.others()):
            self.parts.append(
                copies.send(
                    source_at(node), target.at[place.node], send_sems.at[number], recv_sems.at[number], {"node": node}
                )
            )

    def wait(self):
        for part in self.parts:
            part.wait_recv()


def own_rows(feat):
    return pl.ds(feat * OWN, OWN)


def gather_kernel(
    features_in, weights1, weights2, cotangent_in, degrees_in,
    all_feats, own_feats, all_weights1, all_weights2, spread,
    features, cotangent, degrees, own_weights1, own_weights2, blocks, outgoing,
    gather_send, gather_recv, feat_send, feat_recv, local_sems,
):
    place, copies = Place(), Copies()
    pairs = (
        (features_in, features),
        (weights2, own_weights2),
        (weights1, own_weights1),
        (cotangent_in, cotangent),
        (degrees_in, degrees),
    )
    loads = [pltpu.make_async_copy(pair[0], pair[1], local_sems.at[number]) for number, pair in enumerate(pairs)]
    for load in loads:
        load.start()
    place.greet(place.beside())
    loads[0].wait()
    for block in range(NB):
        blocks[block] = features[:, block * BLK : (block + 1) * BLK]
    gather = Gather(copies, place, blocks, all_feats, gather_send, gather_recv)
    gather.start()
    gather.start_columns()
    loads[3].wait()
    loads[4].wait()
    for block in range(OWN):
        nodes = jnp.transpose(cotangent[block * BLK : (block + 1) * BLK, :].astype(F32))
        degree = degrees[pl.ds(place.feat * OWN + block, 1), :].astype(F32)
        outgoing[:, block] = (nodes / degree).astype(BF16).reshape(FEATS, -1, BLK)
    regroups = [
        Regroup(
            copies, place, lambda to: outgoing.at[to], lambda slot: spread.at[slot], feat_send.at[3], feat_recv.at[3]
        )
    ]
    for number, (weights, target) in enumerate(((own_weights2, all_weights2), (own_weights1, all_weights1))):
        loads[1 + number].wait()
        regroups.append(
            Regroup(
                copies, place, lambda to: weights, lambda slot: target.at[slot], feat_send.at[number], feat_recv.at[number]
            )
        )
    own = pltpu.make_async_copy(blocks, all_feats.at[place.node], local_sems.at[len(pairs)])
    own.start()
    gather.rows()
    gather.near()
    regroups.append(
        Regroup(
            copies, place, lambda to: blocks.at[own_rows(to)], lambda slot: own_feats.at[slot], feat_send.at[2], feat_recv.at[2]
        )
    )
    gather.far()
    for regroup in regroups:
        regroup.wait()
    gather.last()
    own.wait()
    copies.finish()


def plan_groups(counts, groups):
    def row(block, total):
        for part in range(4):
            groups[total + part] = block * 4 + part
        return total + (counts[block] + GROUP - 1) // GROUP

    total = lax.fori_loop(0, NB, row, jnp.int32(0))
    for part in range(BATCH):
        groups[total + part] = 0
    return total


def each_step(counts, groups, tiles, held, tile_sems, clear, work):
    total = plan_groups(counts, groups)
    steps = (total + BATCH - 1) // BATCH

    def fetch(step):
        @pl.when(step < steps)
        def _():
            slot = step % STAGES
            for place in range(BATCH):
                group = groups[step * BATCH + place]
                pltpu.make_async_copy(tiles.at[group], held.at[slot, place], tile_sems.at[slot]).start()

    for step in range(STAGES - 1):
        fetch(step)
    clear()

    def body(step, carry):
        fetch(step + STAGES - 1)
        slot = step % STAGES
        pltpu.make_async_copy(tiles.at[pl.ds(0, BATCH)], held.at[slot], tile_sems.at[slot]).wait()
        entries = []
        for place in range(BATCH):
            group = groups[step * BATCH + place]
            block, first = group // 4, (group % 4) * GROUP
            live = jnp.where(step * BATCH + place < total, counts[block], 0)
            wide = jnp.concatenate([held[slot, place, part] for part in range(GROUP)], axis=1)
            entries.append((block, first, live, wide))
        work(entries)
        return carry

    lax.fori_loop(0, steps, body, jnp.int32(0))


def picked(source, cols, entry):
    block, first, live, wide = entry
    parts = []
    for slot in range(GROUP):
        value = source[cols[first + slot, block]]
        parts.append(jnp.where(first + slot < live, value, jnp.zeros_like(value)))
    return dot(jnp.concatenate(parts, axis=1), wide, ((1,), (1,)))


def load_all(pairs, sems):
    loads = [pltpu.make_async_copy(pair[0], pair[1], sems.at[number]) for number, pair in enumerate(pairs)]
    for load in loads:
        load.start()
    for load in loads:
        load.wait()


def back_kernel(cols_in, counts_in, tiles, spread, back, cols, counts, held, sums, groups, tile_sems, load_sems):
    load_all(((cols_in, cols), (counts_in, counts)), load_sems)

    def clear():
        @pl.loop(0, sums.shape[0] // 16)
        def _(part):
            sums[pl.ds(part * 16, 16)] = jnp.zeros((16,) + sums.shape[1:], F32)

    def work(entries):
        backs = [dot(spread[entry[0]], entry[3], ((1,), (0,))) for entry in entries]
        for (block, first, live, _), product in zip(entries, backs):
            for slot in range(GROUP):
                part = product[:, slot * BLK : (slot + 1) * BLK]
                sums[cols[first + slot, block]] += jnp.where(first + slot < live, part, jnp.zeros_like(part))

    each_step(counts, groups, tiles, held, tile_sems, clear, work)

    @pl.loop(0, sums.shape[0] // 16)
    def _(part):
        rows = pl.ds(part * 16, 16)
        back[rows] = sums[rows].astype(BF16)


def mean_kernel(
    cols_in, counts_in, tiles, source, degrees_in,
    mean,
    cols, counts, degrees, held, sums, groups, tile_sems, load_sems,
):
    load_all(((cols_in, cols), (counts_in, counts), (degrees_in, degrees)), load_sems)

    def clear():
        sums[...] = jnp.zeros_like(sums)

    def work(entries):
        products = [picked(source, cols, entry) for entry in entries]
        for entry, product in zip(entries, products):
            sums[entry[0]] += product

    each_step(counts, groups, tiles, held, tile_sems, clear, work)

    @pl.loop(0, NB)
    def _(block):
        mean[block] = (sums[block] / degrees[pl.ds(block, 1), :].astype(F32)).astype(BF16)


def put_tiles(out, kind, first, value):
    for tile in range(value.shape[0] // 4):
        out[first + tile, kind] = value[tile // 2 * 8 : tile // 2 * 8 + 8, tile % 2 * BLK : tile % 2 * BLK + BLK]


def middle_kernel(
    cols, counts, tiles, all_feats, degrees, back_parts, own_feats, weights1, bias1, weights2, cotangent_in,
    all_hidden, hidden, piece,
    held, cotangent, feat_mean, means, slopes, selves, own_hidden, back, own_back,
    grads, feat_buf, early, early_buf, part, came, bufs,
    gather_send, gather_recv, scatter_send, scatter_recv, feat_send, feat_recv, total_send, total_recv,
    tile_sems, local_sems,
):
    place, copies = Place(), Copies()

    def tile_copy(step):
        slot = step % ROW_STAGES
        return pltpu.make_async_copy(tiles.at[own_rows(place.peer(step + 1))], held.at[slot], tile_sems.at[slot])

    for step in range(ROW_STAGES - 1):
        tile_copy(step).start()
    load = pltpu.make_async_copy(cotangent_in, cotangent, local_sems.at[0])
    load.start()
    place.greet(place.others())

    def regroup(number, source_at, target_at):
        return Regroup(copies, place, source_at, target_at, feat_send.at[number], feat_recv.at[number])

    def mean_copy(step):
        to = place.peer(step + 1)
        return pltpu.make_async_remote_copy(
            src_ref=feat_mean.at[own_rows(to)],
            dst_ref=means.at[place.feat],
            send_sem=feat_send.at[0, step],
            recv_sem=feat_recv.at[0, step],
            device_id={"feat": to},
            device_id_type=MESH,
        )

    def own_blocks(step):
        tile_copy(step).wait()
        for part in range(OWN):
            block = place.peer(step + 1) * OWN + part
            parts = []
            for slot in range(tiles.shape[1]):
                value = all_feats[cols[slot, block]]
                parts.append(jnp.where(slot < counts[block], value, jnp.zeros_like(value)))
            wide = jnp.concatenate([held[step % ROW_STAGES, part, slot] for slot in range(tiles.shape[1])], axis=1)
            total = dot(jnp.concatenate(parts, axis=1), wide, ((1,), (1,)))
            feat_mean[block] = (total / degrees[pl.ds(block, 1), :].astype(F32)).astype(BF16)

    def send_blocks(step, carry):
        @pl.when(step + ROW_STAGES - 1 < FEATS)
        def _():
            tile_copy(step + ROW_STAGES - 1).start()

        own_blocks(step)
        mean_copy(step).start()
        return carry

    scatter = Scatter(copies, place, back_parts, bufs, scatter_send, scatter_recv)
    scatter.start()
    first = weights1[...].reshape(-1, weights1.shape[-1])
    bias = jnp.transpose(jnp.broadcast_to(bias1[...], (BLK, bias1.shape[1])))
    lax.fori_loop(0, 3, send_blocks, jnp.int32(0))
    scatter.direct()
    lax.fori_loop(3, FEATS - 1, send_blocks, jnp.int32(0))
    own_blocks(FEATS - 1)
    means[place.feat] = feat_mean[own_rows(place.feat)]
    scatter.middle()
    for step in range(FEATS - 1):
        mean_copy(step).wait()

    def stack(block):
        parts = []
        for part in range(FEATS):
            parts += [own_feats[part, block], means[part, block]]
        return jnp.concatenate(parts, axis=0)

    for block in range(OWN):
        pre = dot(first, stack(block), ((0,), (0,))) + bias
        sigmoid = jax.nn.sigmoid(pre)
        slopes[:, block * BLK : (block + 1) * BLK] = (sigmoid * (1.0 + pre * (1.0 - sigmoid))).astype(BF16)
        hidden[:, block] = (pre * sigmoid).astype(BF16).reshape(FEATS, -1, BLK)
    to_hidden = regroup(1, lambda to: hidden.at[to], lambda slot: own_hidden.at[own_rows(slot)])
    own_weights = weights2[:, 0].reshape(-1, weights2.shape[-1])
    load.wait()
    selves[...] = dot(own_weights, cotangent[...], ((1,), (1,)))
    all_blocks = jnp.concatenate([hidden[:, block].reshape(-1, BLK) for block in range(OWN)], axis=1)
    total = dot(all_blocks, cotangent[...], ((1,), (0,)))
    early[...] = total.reshape(early.shape)
    to_hidden.wait()
    to_early = regroup(4, lambda to: early.at[to], lambda slot: early_buf.at[slot])
    gather = Gather(copies, place, own_hidden, all_hidden, gather_send, gather_recv)
    own = pltpu.make_async_copy(own_hidden, all_hidden.at[place.node], local_sems.at[1])
    own.start()
    scatter.lines_arrived()
    gather.start()
    scatter.turn()
    scatter.middle2()
    gather.start_columns()
    gather.rows()
    scatter.end(back)
    to_back = regroup(2, lambda to: back.at[own_rows(to)], lambda slot: own_back.at[slot])
    neighbour = weights2[:, 1].reshape(-1, weights2.shape[-1])
    first_stack = jnp.concatenate([stack(block) for block in range(OWN)], axis=1)
    to_back.wait()
    came_back = jnp.concatenate(
        [own_back[:, block].reshape(-1, BLK) for block in range(OWN)], axis=1
    )
    grad = selves[...] + dot(neighbour, came_back, ((1,), (0,)))
    grad = (grad * slopes[...].astype(F32)).astype(BF16)
    first_rows, hid_rows = weights1.shape[1] * weights1.shape[2], weights2.shape[2]
    grads[:, :first_rows] = dot(first_stack, grad, ((1,), (1,))).reshape(FEATS, first_rows, -1)
    all_blocks = jnp.concatenate([hidden[:, block].reshape(-1, BLK) for block in range(OWN)], axis=1)
    grads[:, first_rows:] = dot(all_blocks, came_back, ((1,), (1,))).reshape(FEATS, hid_rows, -1)
    to_total = regroup(3, lambda to: grads.at[to], lambda slot: feat_buf.at[slot])
    part[...] = jnp.zeros_like(part)
    to_early.wait()
    put_tiles(part, 0, 0, sum(early_buf[slot] for slot in range(FEATS)))
    gather.near()
    gather.far((1, 2))
    to_total.wait()
    summed = sum(feat_buf[slot] for slot in range(FEATS))
    put_tiles(part, 0, hid_rows // 4, summed[first_rows:])
    put_tiles(part, 1, 0, summed[:first_rows])
    exchange = Exchange(copies, place, lambda node: part.at[node], came, total_send, total_recv)
    came[place.node] = part[place.node]
    gather.far((3,))
    gather.last()
    exchange.wait()
    piece[...] = sum(came[slot] for slot in range(SIDE * SIDE))
    own.wait()
    copies.finish()


def last_kernel(hidden_mean, piece, means, summed, feat_send, feat_recv, total_send, total_recv):
    place, copies = Place(), Copies()
    place.greet(place.others())
    to_means = Regroup(
        copies, place, lambda to: hidden_mean.at[own_rows(to)], lambda slot: means.at[slot], feat_send, feat_recv
    )
    exchange = Exchange(copies, place, lambda node: piece, summed, total_send, total_recv)
    summed[place.node] = piece[...]
    exchange.wait()
    to_means.wait()
    copies.finish()


def out_kernel(scale, hidden, means, weights2, bias2, summed, hidden_out, grad_second, grad_first):
    second = weights2[...].reshape(-1, weights2.shape[-1])
    for block in range(OWN):
        parts = []
        for part in range(FEATS):
            parts += [hidden[part, block], means[part, block]]
        out = dot(jnp.concatenate(parts, axis=0), second, ((0,), (0,))) + bias2[...]
        hidden_out[block * BLK : (block + 1) * BLK, :] = out.astype(BF16)
    for kind, grad in enumerate((grad_second, grad_first)):
        for tile in range(grad.shape[0] // 8 * 2):
            rows, columns = pl.ds(tile // 2 * 8, 8), pl.ds(tile % 2 * BLK, BLK)
            grad[rows, columns] = summed[tile, kind] * scale


def limit(mib, collective_id=None):
    if collective_id is None:
        return pltpu.CompilerParams(vmem_limit_bytes=mib * 1024 * 1024)
    return pltpu.CompilerParams(
        collective_id=collective_id, has_side_effects=True, vmem_limit_bytes=mib * 1024 * 1024
    )


def shape(*dims, dtype=BF16):
    return jax.ShapeDtypeStruct(dims, dtype)


def buf(*dims, dtype=BF16):
    return pltpu.VMEM(dims, dtype)


def dma(*dims):
    return pltpu.SemaphoreType.DMA(dims)


def in_hbm(array):
    return pltpu.with_memory_space_constraint(array, pltpu.HBM)


def shards(
    features, tile_cols, tile_counts, tiles, degrees, weights1, bias1, weights2, bias2, cotangent
):
    feat_part = features.shape[0]
    hid_part = weights2.shape[1]
    width = weights2.shape[2]
    shard_total = lax.axis_size("node")
    block_total = shard_total * NB
    scale = 1.0 / math.sqrt(features.shape[1] * shard_total)
    own_nodes = OWN * BLK
    degree_rows = degrees.reshape(NB, BLK)
    groups = tiles.reshape(NB * tiles.shape[1] // GROUP, GROUP, BLK, BLK)

    all_feats, own_feats, all_weights1, all_weights2, spread = pl.pallas_call(
        gather_kernel,
        out_shape=(
            shape(shard_total, NB, feat_part, BLK),
            shape(FEATS, OWN, feat_part, BLK),
            shape(FEATS, 2, feat_part, width),
            shape(FEATS, 2, hid_part, width),
            shape(FEATS, OWN, hid_part, BLK),
        ),
        in_specs=[HBM] * 5,
        out_specs=(ANY, VMEM, VMEM, VMEM, VMEM),
        scratch_shapes=[
            buf(*features.shape),
            buf(own_nodes, width),
            buf(NB, BLK, dtype=jnp.int32),
            buf(*weights1.shape),
            buf(*weights2.shape),
            buf(NB, feat_part, BLK),
            buf(FEATS, OWN, hid_part, BLK),
            dma(2, 5, 4),
            dma(2, 5, 4),
            dma(4, FEATS - 1),
            dma(4, FEATS - 1),
            dma(6),
        ],
        compiler_params=limit(12, 1),
        name="gather_features",
    )(*[in_hbm(array) for array in (features, weights1, weights2, cotangent, degree_rows)])

    held = buf(STAGES, BATCH, GROUP, BLK, BLK)
    planned = pltpu.SMEM((NB * 4 + 2 * BATCH,), jnp.int32)
    slot_cols = tile_cols.T
    listed = [pltpu.SMEM((tiles.shape[1], NB), jnp.int32), pltpu.SMEM((NB,), jnp.int32)]
    back_parts = pl.pallas_call(
        back_kernel,
        out_shape=shape(block_total, hid_part, BLK),
        in_specs=[HBM, HBM, HBM, VMEM],
        out_specs=VMEM,
        scratch_shapes=[
            *listed,
            held,
            buf(block_total, hid_part, BLK, dtype=F32),
            planned,
            dma(STAGES),
            dma(2),
        ],
        compiler_params=limit(28),
        name="aggregate_back",
    )(in_hbm(slot_cols), in_hbm(tile_counts), in_hbm(groups), spread.reshape(NB, hid_part, BLK))

    row = (SIDE, HALF, hid_part, BLK)
    part_row = (SIDE, QUARTER, hid_part, BLK)
    middle_bufs = (
        buf(2, 2, *part_row),
        buf(2, 2, *row),
        buf(2, 2, *part_row),
        buf(2, *row),
        buf(2, 2, *part_row[1:]),
        buf(2, 2, *row[1:]),
        buf(2, 2, *part_row[1:]),
    )
    first_rows, second_rows = 2 * feat_part, 2 * hid_part
    pieces = (shard_total, 2, 8, BLK)
    all_hidden, hidden, piece = pl.pallas_call(
        middle_kernel,
        out_shape=(
            shape(shard_total, NB, hid_part, BLK),
            shape(FEATS, OWN, hid_part, BLK),
            shape(*pieces[1:], dtype=F32),
        ),
        in_specs=[SMEM, SMEM, HBM] + [VMEM] * 7 + [HBM],
        out_specs=(ANY, VMEM, VMEM),
        scratch_shapes=[
            buf(ROW_STAGES, OWN, *tiles.shape[1:]),
            buf(own_nodes, width),
            buf(NB, feat_part, BLK),
            buf(FEATS, OWN, feat_part, BLK),
            buf(width, own_nodes),
            buf(width, own_nodes, dtype=F32),
            buf(NB, hid_part, BLK),
            buf(NB, hid_part, BLK),
            buf(FEATS, OWN, hid_part, BLK),
            buf(FEATS, first_rows + hid_part, width, dtype=F32),
            buf(FEATS, first_rows + hid_part, width, dtype=F32),
            buf(FEATS, hid_part, width, dtype=F32),
            buf(FEATS, hid_part, width, dtype=F32),
            buf(*pieces, dtype=F32),
            buf(*pieces, dtype=F32),
            middle_bufs,
            dma(2, 5, 4),
            dma(2, 5, 4),
            dma(2, 2, 2, 3),
            dma(2, 2, 2, 3),
            dma(5, FEATS - 1),
            dma(5, FEATS - 1),
            dma(shard_total - 1),
            dma(shard_total - 1),
            dma(ROW_STAGES),
            dma(2),
        ],
        compiler_params=limit(36, 2),
        name="first_layer",
    )(
        slot_cols,
        tile_counts,
        in_hbm(tiles),
        all_feats.reshape(block_total, feat_part, BLK),
        degree_rows,
        back_parts.reshape(SIDE, SIDE, NB, hid_part, BLK),
        own_feats,
        all_weights1,
        bias1.reshape(1, width),
        all_weights2,
        in_hbm(cotangent),
    )

    hidden_mean = pl.pallas_call(
        mean_kernel,
        out_shape=shape(NB, hid_part, BLK),
        in_specs=[HBM, HBM, HBM, VMEM, HBM],
        out_specs=VMEM,
        scratch_shapes=[
            *listed,
            buf(NB, BLK, dtype=jnp.int32),
            held,
            buf(NB, hid_part, BLK, dtype=F32),
            planned,
            dma(STAGES),
            dma(3),
        ],
        compiler_params=limit(20),
        name="aggregate_hidden",
    )(
        in_hbm(slot_cols),
        in_hbm(tile_counts),
        in_hbm(groups),
        all_hidden.reshape(block_total, hid_part, BLK),
        in_hbm(degree_rows),
    )

    means, summed = pl.pallas_call(
        last_kernel,
        out_shape=(shape(FEATS, OWN, hid_part, BLK), shape(*pieces, dtype=F32)),
        in_specs=[VMEM] * 2,
        out_specs=(VMEM, VMEM),
        scratch_shapes=[dma(FEATS - 1), dma(FEATS - 1), dma(shard_total - 1), dma(shard_total - 1)],
        compiler_params=limit(8, 3),
        name="regroup_mean",
    )(hidden_mean, piece)
    hidden_out, grad_second, grad_first = pl.pallas_call(
        functools.partial(out_kernel, scale),
        out_shape=(
            shape(own_nodes, width),
            shape(second_rows, width, dtype=F32),
            shape(first_rows, width, dtype=F32),
        ),
        in_specs=[VMEM] * 5,
        out_specs=(VMEM, VMEM, VMEM),
        compiler_params=limit(8),
        name="second_layer",
    )(hidden, means, all_weights2, bias2.reshape(1, width), summed)
    return (
        hidden_out,
        grad_second.reshape(2, hid_part, width),
        grad_first.reshape(2, feat_part, width),
    )


def solution(mesh):
    return jax.shard_map(
        shards,
        mesh=mesh,
        in_specs=(
            P("feat", "node"),
            P("node", None),
            P("node"),
            P("node", None, None, None),
            P("node"),
            P(None, "feat", None),
            P(),
            P(None, "feat", None),
            P(),
            P(("node", "feat"), None),
        ),
        out_specs=(P(("node", "feat"), None), P(None, "feat", None), P(None, "feat", None)),
        check_vma=False,
    )
```

```python
import functools
import math

import jax
import jax.numpy as jnp
from jax import lax
from jax.experimental import pallas as pl
from jax.experimental.pallas import tpu as pltpu
from jax.sharding import PartitionSpec as P

MESH = pl.DeviceIdType.MESH
BF16 = jnp.bfloat16
F32 = jnp.float32
FEATS = 8
SIDE = 4
BLK = 128
NB = 48
OWN = NB // FEATS
HALF, QUARTER = NB // 2, NB // 4
GROUP = 4
BATCH = 8
STAGES = 4
ROW_STAGES = 3
AHEAD = (0, -1, 1, 2)
VMEM = pl.BlockSpec(memory_space=pltpu.VMEM)
SMEM = pl.BlockSpec(memory_space=pltpu.SMEM)
ANY = pl.BlockSpec(memory_space=pl.ANY)
HBM = pl.BlockSpec(memory_space=pltpu.HBM)


def dot(left, right, dims):
    return lax.dot_general(left, right, (dims, ((), ())), preferred_element_type=F32)


class Place:
    def __init__(self):
        self.feat = lax.axis_index("feat")
        self.node = lax.axis_index("node")
        self.x = self.node // SIDE
        self.z = self.node % SIDE

    def peer(self, step):
        return (self.feat + step + FEATS) % FEATS

    def shift(self, dx, dz):
        return ((self.x + dx + SIDE) % SIDE) * SIDE + (self.z + dz + SIDE) % SIDE

    def beside(self):
        return [self.shift(dx, dz) for dx, dz in ((1, 0), (-1, 0), (0, 1), (0, -1))]

    def others(self):
        total = SIDE * SIDE
        return [(self.node + step) % total for step in range(1, total)]

    def turned(self, half, first, second):
        return self.shift(first, second) if half == 0 else self.shift(second, first)

    def greet(self, nodes):
        barrier = pltpu.get_barrier_semaphore()
        others = [{"feat": self.peer(step)} for step in range(1, FEATS)]
        others += [{"node": node} for node in nodes]
        for other in others:
            pl.semaphore_signal(barrier, inc=1, device_id=other, device_id_type=MESH)
        pl.semaphore_wait(barrier, len(others))


class Copies:
    def __init__(self):
        self.sent = []

    def send(self, source, target, send_sem, recv_sem, device):
        copy = pltpu.make_async_remote_copy(
            src_ref=source,
            dst_ref=target,
            send_sem=send_sem,
            recv_sem=recv_sem,
            device_id=device,
            device_id_type=MESH,
        )
        copy.start()
        self.sent.append(copy)
        return copy

    def finish(self):
        for copy in self.sent:
            copy.wait_send()


class Regroup:
    def __init__(self, copies, place, source_at, target_at, send_sems, recv_sems):
        self.parts = []
        for step in range(1, FEATS):
            to = place.peer(step)
            self.parts.append(
                copies.send(
                    source_at(to),
                    target_at(place.feat),
                    send_sems.at[step - 1],
                    recv_sems.at[step - 1],
                    {"feat": to},
                )
            )
        target_at(place.feat)[...] = source_at(place.feat)[...]

    def wait(self):
        for part in self.parts:
            part.wait_recv()


class Gather:
    def __init__(self, copies, place, own, out, send_sems, recv_sems):
        self.copies, self.place, self.own, self.out = copies, place, own, out
        self.send_sems, self.recv_sems = send_sems, recv_sems
        self.made = {}

    def _send(self, half, unit, role, source, target, first, second):
        place = self.place
        self.made[half, unit, role] = self.copies.send(
            source,
            target,
            self.send_sems.at[half, unit, role],
            self.recv_sems.at[half, unit, role],
            {"node": place.turned(half, first, second)},
        )

    def full(self, half, unit):
        rows = pl.ds(half * HALF, HALF)
        ahead = 0 if unit == SIDE else AHEAD[unit]
        shard = self.place.turned(half, ahead, 0)
        source = self.own.at[rows] if ahead == 0 else self.out.at[shard, rows]
        for role, way in ((0, 1), (1, -1)):
            move = (way, 0) if unit == SIDE else (0, way)
            self._send(half, unit, role, source, self.out.at[shard, rows], *move)

    def forward(self, half, unit, role):
        way = 1 if role == 0 else -1
        self.made[half, unit, role].wait_recv()
        rows = pl.ds(half * HALF + role * QUARTER, QUARTER)
        if unit == SIDE:
            shard, move = self.place.turned(half, -way, 0), (way, 0)
        else:
            shard, move = self.place.turned(half, AHEAD[unit], -way), (0, way)
        part = self.out.at[shard, rows]
        self._send(half, unit, role + 2, part, part, *move)

    def arrived(self, half, unit):
        for role in (2, 3):
            self.made[half, unit, role].wait_recv()

    def start(self):
        for half in range(2):
            self.full(half, SIDE)

    def start_columns(self):
        for half in range(2):
            self.full(half, 0)

    def rows(self):
        for role in range(2):
            for half in range(2):
                self.forward(half, SIDE, role)
                self.full(half, role + 1)

    def near(self):
        for role in range(2):
            for half in range(2):
                self.forward(half, 0, role)
        for half in range(2):
            self.arrived(half, SIDE)
            self.full(half, 3)

    def far(self, units=(1, 2, 3)):
        for unit in units:
            for role in range(2):
                for half in range(2):
                    self.forward(half, unit, role)

    def last(self):
        for unit in range(SIDE):
            for half in range(2):
                self.arrived(half, unit)


class Scatter:
    def __init__(self, copies, place, parts, bufs, send_sems, recv_sems):
        self.copies, self.place, self.parts = copies, place, parts
        self.pass1, self.got1, self.sum1, self.half1, self.pass2, self.got2, self.sum2 = bufs
        self.send_sems, self.recv_sems = send_sems, recv_sems
        self.made = {}

    def _send(self, half, phase, side, kind, source, target):
        way = 1 if side == 0 else -1
        first, second = (way, 0) if phase == 0 else (0, way)
        self.made[half, phase, side, kind] = self.copies.send(
            source,
            target,
            self.send_sems.at[half, phase, side, kind],
            self.recv_sems.at[half, phase, side, kind],
            {"node": self.place.turned(half, first, second)},
        )

    def _line(self, half, ahead, quarter=None):
        rows = pl.ds(half * HALF, HALF)
        if quarter is not None:
            rows = pl.ds(half * HALF + quarter * QUARTER, QUARTER)
        if half == 0:
            return self.parts.at[(self.place.x + ahead + SIDE) % SIDE, :, rows]
        return self.parts.at[:, (self.place.z + ahead + SIDE) % SIDE, rows]

    def _unit(self, half, ahead, quarter):
        at = self.place.z if half == 0 else self.place.x
        rows = pl.ds(quarter * QUARTER, QUARTER)
        return self.half1.at[half, (at + ahead + SIDE) % SIDE, rows]

    def start(self):
        for half in range(2):
            for side, way in ((0, 1), (1, -1)):
                self._send(half, 0, side, 0, self._line(half, 2 * way, side), self.pass1.at[half, side])

    def direct(self):
        for half in range(2):
            for side, way in ((0, 1), (1, -1)):
                rows = pl.ds((1 - side) * QUARTER, QUARTER)
                self._send(half, 0, side, 1, self._line(half, way, 1 - side), self.got1.at[half, side, :, rows])

    def middle(self):
        for side, way in ((0, 1), (1, -1)):
            for half in range(2):
                self.made[half, 0, side, 0].wait_recv()
                mine, came, total = self._line(half, way, side), self.pass1.at[half, side], self.sum1.at[half, side]

                @pl.loop(0, SIDE)
                def _(shard):
                    total[shard] = (mine[shard].astype(F32) + came[shard].astype(F32)).astype(BF16)

                rows = pl.ds(side * QUARTER, QUARTER)
                self._send(half, 0, side, 2, total, self.got1.at[half, side, :, rows])

    def lines_arrived(self):
        for half in range(2):
            for side in range(2):
                for kind in (1, 2):
                    self.made[half, 0, side, kind].wait_recv()

    def turn(self):
        for half in range(2):
            mine, left, right, total = self._line(half, 0), self.got1.at[half, 0], self.got1.at[half, 1], self.half1.at[half]

            @pl.loop(0, SIDE)
            def _(shard):
                near = left[shard].astype(F32) + right[shard].astype(F32)
                total[shard] = (mine[shard].astype(F32) + near).astype(BF16)

            for side, way in ((0, 1), (1, -1)):
                self._send(half, 1, side, 0, self._unit(half, 2 * way, side), self.pass2.at[half, side])
            for side, way in ((0, 1), (1, -1)):
                rows = pl.ds((1 - side) * QUARTER, QUARTER)
                self._send(half, 1, side, 1, self._unit(half, way, 1 - side), self.got2.at[half, side, rows])

    def middle2(self):
        for side, way in ((0, 1), (1, -1)):
            for half in range(2):
                self.made[half, 1, side, 0].wait_recv()
                total = self.sum2.at[half, side]
                mine, came = self._unit(half, way, side)[...], self.pass2[half, side]
                total[...] = (mine.astype(F32) + came.astype(F32)).astype(BF16)
                rows = pl.ds(side * QUARTER, QUARTER)
                self._send(half, 1, side, 2, total, self.got2.at[half, side, rows])

    def end(self, out):
        for half in range(2):
            for side in range(2):
                for kind in (1, 2):
                    self.made[half, 1, side, kind].wait_recv()
            for quarter in range(2):
                rows = pl.ds(quarter * QUARTER, QUARTER)
                near = self.got2[half, 0, rows].astype(F32) + self.got2[half, 1, rows].astype(F32)
                total = self._unit(half, 0, quarter)[...].astype(F32) + near
                out[pl.ds(half * HALF + quarter * QUARTER, QUARTER)] = total.astype(BF16)


class Rows:
    def __init__(self, place, cols, counts, tiles, source, degrees, mean, means, held, send_sems, recv_sems, tile_sems):
        self.place, self.cols, self.counts, self.tiles, self.source = place, cols, counts, tiles, source
        self.degrees, self.mean, self.means, self.held = degrees, mean, means, held
        self.send_sems, self.recv_sems, self.tile_sems = send_sems, recv_sems, tile_sems
        for step in range(ROW_STAGES - 1):
            self.fetch(step).start()

    def fetch(self, step):
        slot = step % ROW_STAGES
        rows = own_rows(self.place.peer(step + 1))
        return pltpu.make_async_copy(self.tiles.at[rows], self.held.at[slot], self.tile_sems.at[slot])

    def give(self, step):
        to = self.place.peer(step + 1)
        return pltpu.make_async_remote_copy(
            src_ref=self.mean.at[own_rows(to)],
            dst_ref=self.means.at[self.place.feat],
            send_sem=self.send_sems.at[step],
            recv_sem=self.recv_sems.at[step],
            device_id={"feat": to},
            device_id_type=MESH,
        )

    def work(self, step):
        self.fetch(step).wait()
        slots = self.tiles.shape[1]
        for part in range(OWN):
            block = self.place.peer(step + 1) * OWN + part
            parts = []
            for slot in range(slots):
                value = self.source[self.cols[slot, block]]
                parts.append(jnp.where(slot < self.counts[block], value, jnp.zeros_like(value)))
            wide = jnp.concatenate([self.held[step % ROW_STAGES, part, slot] for slot in range(slots)], axis=1)
            total = dot(jnp.concatenate(parts, axis=1), wide, ((1,), (1,)))
            self.mean[block] = (total / self.degrees[pl.ds(block, 1), :].astype(F32)).astype(BF16)

    def run(self, first, last):
        def body(step, carry):
            @pl.when(step + ROW_STAGES - 1 < FEATS)
            def _():
                self.fetch(step + ROW_STAGES - 1).start()

            self.work(step)
            self.give(step).start()
            return carry

        lax.fori_loop(first, last, body, jnp.int32(0))

    def own(self):
        self.work(FEATS - 1)
        self.means[self.place.feat] = self.mean[own_rows(self.place.feat)]

    def wait(self):
        for step in range(FEATS - 1):
            self.give(step).wait()


class Exchange:
    def __init__(self, copies, place, source_at, target, send_sems, recv_sems):
        self.parts = []
        for number, node in enumerate(place.others()):
            self.parts.append(
                copies.send(
                    source_at(node), target.at[place.node], send_sems.at[number], recv_sems.at[number], {"node": node}
                )
            )

    def wait(self):
        for part in self.parts:
            part.wait_recv()


def own_rows(feat):
    return pl.ds(feat * OWN, OWN)


def gather_kernel(
    features_in, weights1, weights2, cotangent_in, degrees_in,
    all_feats, own_feats, all_weights1, all_weights2, spread,
    features, cotangent, degrees, own_weights1, own_weights2, blocks, outgoing,
    gather_send, gather_recv, feat_send, feat_recv, local_sems,
):
    place, copies = Place(), Copies()
    pairs = (
        (features_in, features),
        (weights2, own_weights2),
        (weights1, own_weights1),
        (cotangent_in, cotangent),
        (degrees_in, degrees),
    )
    loads = [pltpu.make_async_copy(pair[0], pair[1], local_sems.at[number]) for number, pair in enumerate(pairs)]
    for load in loads:
        load.start()
    place.greet(place.beside())
    loads[0].wait()
    for block in range(NB):
        blocks[block] = features[:, block * BLK : (block + 1) * BLK]
    gather = Gather(copies, place, blocks, all_feats, gather_send, gather_recv)
    gather.start()
    gather.start_columns()
    loads[3].wait()
    loads[4].wait()
    for block in range(OWN):
        nodes = jnp.transpose(cotangent[block * BLK : (block + 1) * BLK, :].astype(F32))
        degree = degrees[pl.ds(place.feat * OWN + block, 1), :].astype(F32)
        outgoing[:, block] = (nodes / degree).astype(BF16).reshape(FEATS, -1, BLK)
    regroups = [
        Regroup(
            copies, place, lambda to: outgoing.at[to], lambda slot: spread.at[slot], feat_send.at[3], feat_recv.at[3]
        )
    ]
    for number, (weights, target) in enumerate(((own_weights2, all_weights2), (own_weights1, all_weights1))):
        loads[1 + number].wait()
        regroups.append(
            Regroup(
                copies, place, lambda to: weights, lambda slot: target.at[slot], feat_send.at[number], feat_recv.at[number]
            )
        )
    own = pltpu.make_async_copy(blocks, all_feats.at[place.node], local_sems.at[len(pairs)])
    own.start()
    gather.rows()
    gather.near()
    regroups.append(
        Regroup(
            copies, place, lambda to: blocks.at[own_rows(to)], lambda slot: own_feats.at[slot], feat_send.at[2], feat_recv.at[2]
        )
    )
    gather.far()
    for regroup in regroups:
        regroup.wait()
    gather.last()
    own.wait()
    copies.finish()


def plan_groups(counts, groups):
    def row(block, total):
        for part in range(4):
            groups[total + part] = block * 4 + part
        return total + (counts[block] + GROUP - 1) // GROUP

    total = lax.fori_loop(0, NB, row, jnp.int32(0))
    for part in range(BATCH):
        groups[total + part] = 0
    return total


def each_step(counts, groups, tiles, held, tile_sems, clear, work):
    total = plan_groups(counts, groups)
    steps = (total + BATCH - 1) // BATCH

    def fetch(step):
        @pl.when(step < steps)
        def _():
            slot = step % STAGES
            for place in range(BATCH):
                group = groups[step * BATCH + place]
                pltpu.make_async_copy(tiles.at[group], held.at[slot, place], tile_sems.at[slot]).start()

    for step in range(STAGES - 1):
        fetch(step)
    clear()

    def body(step, carry):
        fetch(step + STAGES - 1)
        slot = step % STAGES
        pltpu.make_async_copy(tiles.at[pl.ds(0, BATCH)], held.at[slot], tile_sems.at[slot]).wait()
        entries = []
        for place in range(BATCH):
            group = groups[step * BATCH + place]
            block, first = group // 4, (group % 4) * GROUP
            live = jnp.where(step * BATCH + place < total, counts[block], 0)
            wide = jnp.concatenate([held[slot, place, part] for part in range(GROUP)], axis=1)
            entries.append((block, first, live, wide))
        work(entries)
        return carry

    lax.fori_loop(0, steps, body, jnp.int32(0))


def load_all(pairs, sems):
    loads = [pltpu.make_async_copy(pair[0], pair[1], sems.at[number]) for number, pair in enumerate(pairs)]
    for load in loads:
        load.start()
    for load in loads:
        load.wait()


def back_kernel(cols_in, counts_in, tiles, spread, back, cols, counts, held, sums, groups, tile_sems, load_sems):
    load_all(((cols_in, cols), (counts_in, counts)), load_sems)

    def clear():
        @pl.loop(0, sums.shape[0] // 16)
        def _(part):
            sums[pl.ds(part * 16, 16)] = jnp.zeros((16,) + sums.shape[1:], F32)

    def work(entries):
        backs = [dot(spread[entry[0]], entry[3], ((1,), (0,))) for entry in entries]
        for (block, first, live, _), product in zip(entries, backs):
            for slot in range(GROUP):
                part = product[:, slot * BLK : (slot + 1) * BLK]
                sums[cols[first + slot, block]] += jnp.where(first + slot < live, part, jnp.zeros_like(part))

    each_step(counts, groups, tiles, held, tile_sems, clear, work)

    @pl.loop(0, sums.shape[0] // 16)
    def _(part):
        rows = pl.ds(part * 16, 16)
        back[rows] = sums[rows].astype(BF16)


def put_tiles(out, kind, first, value):
    for tile in range(value.shape[0] // 4):
        out[first + tile, kind] = value[tile // 2 * 8 : tile // 2 * 8 + 8, tile % 2 * BLK : tile % 2 * BLK + BLK]


def middle_kernel(
    cols, counts, tiles, all_feats, degrees, back_parts, own_feats, weights1, bias1, weights2, cotangent_in,
    all_hidden, hidden, piece,
    held, cotangent, feat_mean, means, slopes, selves, own_hidden, back, own_back,
    grads, feat_buf, early, early_buf, part, came, bufs,
    gather_send, gather_recv, scatter_send, scatter_recv, feat_send, feat_recv, total_send, total_recv,
    tile_sems, local_sems,
):
    place, copies = Place(), Copies()

    rows = Rows(
        place, cols, counts, tiles, all_feats, degrees, feat_mean, means, held, feat_send.at[0], feat_recv.at[0], tile_sems
    )
    load = pltpu.make_async_copy(cotangent_in, cotangent, local_sems.at[0])
    load.start()
    place.greet(place.others())

    def regroup(number, source_at, target_at):
        return Regroup(copies, place, source_at, target_at, feat_send.at[number], feat_recv.at[number])

    scatter = Scatter(copies, place, back_parts, bufs, scatter_send, scatter_recv)
    scatter.start()
    first = weights1[...].reshape(-1, weights1.shape[-1])
    bias = jnp.transpose(jnp.broadcast_to(bias1[...], (BLK, bias1.shape[1])))
    rows.run(0, 3)
    scatter.direct()
    rows.run(3, FEATS - 1)
    rows.own()
    scatter.middle()
    rows.wait()

    def stack(block):
        parts = []
        for part in range(FEATS):
            parts += [own_feats[part, block], means[part, block]]
        return jnp.concatenate(parts, axis=0)

    for block in range(OWN):
        pre = dot(first, stack(block), ((0,), (0,))) + bias
        sigmoid = jax.nn.sigmoid(pre)
        slopes[:, block * BLK : (block + 1) * BLK] = (sigmoid * (1.0 + pre * (1.0 - sigmoid))).astype(BF16)
        hidden[:, block] = (pre * sigmoid).astype(BF16).reshape(FEATS, -1, BLK)
    to_hidden = regroup(1, lambda to: hidden.at[to], lambda slot: own_hidden.at[own_rows(slot)])
    own_weights = weights2[:, 0].reshape(-1, weights2.shape[-1])
    load.wait()
    selves[...] = dot(own_weights, cotangent[...], ((1,), (1,)))
    all_blocks = jnp.concatenate([hidden[:, block].reshape(-1, BLK) for block in range(OWN)], axis=1)
    total = dot(all_blocks, cotangent[...], ((1,), (0,)))
    early[...] = total.reshape(early.shape)
    to_hidden.wait()
    to_early = regroup(4, lambda to: early.at[to], lambda slot: early_buf.at[slot])
    gather = Gather(copies, place, own_hidden, all_hidden, gather_send, gather_recv)
    own = pltpu.make_async_copy(own_hidden, all_hidden.at[place.node], local_sems.at[1])
    own.start()
    scatter.lines_arrived()
    gather.start()
    scatter.turn()
    scatter.middle2()
    gather.start_columns()
    gather.rows()
    scatter.end(back)
    to_back = regroup(2, lambda to: back.at[own_rows(to)], lambda slot: own_back.at[slot])
    neighbour = weights2[:, 1].reshape(-1, weights2.shape[-1])
    first_stack = jnp.concatenate([stack(block) for block in range(OWN)], axis=1)
    to_back.wait()
    came_back = jnp.concatenate(
        [own_back[:, block].reshape(-1, BLK) for block in range(OWN)], axis=1
    )
    grad = selves[...] + dot(neighbour, came_back, ((1,), (0,)))
    grad = (grad * slopes[...].astype(F32)).astype(BF16)
    first_rows, hid_rows = weights1.shape[1] * weights1.shape[2], weights2.shape[2]
    grads[:, :first_rows] = dot(first_stack, grad, ((1,), (1,))).reshape(FEATS, first_rows, -1)
    all_blocks = jnp.concatenate([hidden[:, block].reshape(-1, BLK) for block in range(OWN)], axis=1)
    grads[:, first_rows:] = dot(all_blocks, came_back, ((1,), (1,))).reshape(FEATS, hid_rows, -1)
    to_total = regroup(3, lambda to: grads.at[to], lambda slot: feat_buf.at[slot])
    part[...] = jnp.zeros_like(part)
    to_early.wait()
    put_tiles(part, 0, 0, sum(early_buf[slot] for slot in range(FEATS)))
    gather.near()
    gather.far((1, 2))
    to_total.wait()
    summed = sum(feat_buf[slot] for slot in range(FEATS))
    put_tiles(part, 0, hid_rows // 4, summed[first_rows:])
    put_tiles(part, 1, 0, summed[:first_rows])
    exchange = Exchange(copies, place, lambda node: part.at[node], came, total_send, total_recv)
    came[place.node] = part[place.node]
    gather.far((3,))
    gather.last()
    exchange.wait()
    piece[...] = sum(came[slot] for slot in range(SIDE * SIDE))
    own.wait()
    copies.finish()


def last_kernel(
    cols, counts, tiles, all_hidden, degrees, piece,
    means, summed,
    held, hidden_mean, feat_send, feat_recv, total_send, total_recv, tile_sems,
):
    place, copies = Place(), Copies()
    rows = Rows(
        place, cols, counts, tiles, all_hidden, degrees, hidden_mean, means, held, feat_send, feat_recv, tile_sems
    )
    place.greet(place.others())
    exchange = Exchange(copies, place, lambda node: piece, summed, total_send, total_recv)
    summed[place.node] = piece[...]
    rows.run(0, FEATS - 1)
    rows.own()
    rows.wait()
    exchange.wait()
    copies.finish()


def out_kernel(scale, hidden, means, weights2, bias2, summed, hidden_out, grad_second, grad_first):
    second = weights2[...].reshape(-1, weights2.shape[-1])
    for block in range(OWN):
        parts = []
        for part in range(FEATS):
            parts += [hidden[part, block], means[part, block]]
        out = dot(jnp.concatenate(parts, axis=0), second, ((0,), (0,))) + bias2[...]
        hidden_out[block * BLK : (block + 1) * BLK, :] = out.astype(BF16)
    for kind, grad in enumerate((grad_second, grad_first)):
        for tile in range(grad.shape[0] // 8 * 2):
            rows, columns = pl.ds(tile // 2 * 8, 8), pl.ds(tile % 2 * BLK, BLK)
            grad[rows, columns] = summed[tile, kind] * scale


def limit(mib, collective_id=None):
    if collective_id is None:
        return pltpu.CompilerParams(vmem_limit_bytes=mib * 1024 * 1024)
    return pltpu.CompilerParams(
        collective_id=collective_id, has_side_effects=True, vmem_limit_bytes=mib * 1024 * 1024
    )


def shape(*dims, dtype=BF16):
    return jax.ShapeDtypeStruct(dims, dtype)


def buf(*dims, dtype=BF16):
    return pltpu.VMEM(dims, dtype)


def dma(*dims):
    return pltpu.SemaphoreType.DMA(dims)


def in_hbm(array):
    return pltpu.with_memory_space_constraint(array, pltpu.HBM)


def shards(
    features, tile_cols, tile_counts, tiles, degrees, weights1, bias1, weights2, bias2, cotangent
):
    feat_part = features.shape[0]
    hid_part = weights2.shape[1]
    width = weights2.shape[2]
    shard_total = lax.axis_size("node")
    block_total = shard_total * NB
    scale = 1.0 / math.sqrt(features.shape[1] * shard_total)
    own_nodes = OWN * BLK
    degree_rows = degrees.reshape(NB, BLK)
    groups = tiles.reshape(NB * tiles.shape[1] // GROUP, GROUP, BLK, BLK)

    all_feats, own_feats, all_weights1, all_weights2, spread = pl.pallas_call(
        gather_kernel,
        out_shape=(
            shape(shard_total, NB, feat_part, BLK),
            shape(FEATS, OWN, feat_part, BLK),
            shape(FEATS, 2, feat_part, width),
            shape(FEATS, 2, hid_part, width),
            shape(FEATS, OWN, hid_part, BLK),
        ),
        in_specs=[HBM] * 5,
        out_specs=(ANY, VMEM, VMEM, VMEM, VMEM),
        scratch_shapes=[
            buf(*features.shape),
            buf(own_nodes, width),
            buf(NB, BLK, dtype=jnp.int32),
            buf(*weights1.shape),
            buf(*weights2.shape),
            buf(NB, feat_part, BLK),
            buf(FEATS, OWN, hid_part, BLK),
            dma(2, 5, 4),
            dma(2, 5, 4),
            dma(4, FEATS - 1),
            dma(4, FEATS - 1),
            dma(6),
        ],
        compiler_params=limit(12, 1),
        name="gather_features",
    )(*[in_hbm(array) for array in (features, weights1, weights2, cotangent, degree_rows)])

    held = buf(STAGES, BATCH, GROUP, BLK, BLK)
    planned = pltpu.SMEM((NB * 4 + 2 * BATCH,), jnp.int32)
    slot_cols = tile_cols.T
    listed = [pltpu.SMEM((tiles.shape[1], NB), jnp.int32), pltpu.SMEM((NB,), jnp.int32)]
    back_parts = pl.pallas_call(
        back_kernel,
        out_shape=shape(block_total, hid_part, BLK),
        in_specs=[HBM, HBM, HBM, VMEM],
        out_specs=VMEM,
        scratch_shapes=[
            *listed,
            held,
            buf(block_total, hid_part, BLK, dtype=F32),
            planned,
            dma(STAGES),
            dma(2),
        ],
        compiler_params=limit(28),
        name="aggregate_back",
    )(in_hbm(slot_cols), in_hbm(tile_counts), in_hbm(groups), spread.reshape(NB, hid_part, BLK))

    row = (SIDE, HALF, hid_part, BLK)
    part_row = (SIDE, QUARTER, hid_part, BLK)
    middle_bufs = (
        buf(2, 2, *part_row),
        buf(2, 2, *row),
        buf(2, 2, *part_row),
        buf(2, *row),
        buf(2, 2, *part_row[1:]),
        buf(2, 2, *row[1:]),
        buf(2, 2, *part_row[1:]),
    )
    first_rows, second_rows = 2 * feat_part, 2 * hid_part
    pieces = (shard_total, 2, 8, BLK)
    all_hidden, hidden, piece = pl.pallas_call(
        middle_kernel,
        out_shape=(
            shape(shard_total, NB, hid_part, BLK),
            shape(FEATS, OWN, hid_part, BLK),
            shape(*pieces[1:], dtype=F32),
        ),
        in_specs=[SMEM, SMEM, HBM] + [VMEM] * 7 + [HBM],
        out_specs=(ANY, VMEM, VMEM),
        scratch_shapes=[
            buf(ROW_STAGES, OWN, *tiles.shape[1:]),
            buf(own_nodes, width),
            buf(NB, feat_part, BLK),
            buf(FEATS, OWN, feat_part, BLK),
            buf(width, own_nodes),
            buf(width, own_nodes, dtype=F32),
            buf(NB, hid_part, BLK),
            buf(NB, hid_part, BLK),
            buf(FEATS, OWN, hid_part, BLK),
            buf(FEATS, first_rows + hid_part, width, dtype=F32),
            buf(FEATS, first_rows + hid_part, width, dtype=F32),
            buf(FEATS, hid_part, width, dtype=F32),
            buf(FEATS, hid_part, width, dtype=F32),
            buf(*pieces, dtype=F32),
            buf(*pieces, dtype=F32),
            middle_bufs,
            dma(2, 5, 4),
            dma(2, 5, 4),
            dma(2, 2, 2, 3),
            dma(2, 2, 2, 3),
            dma(5, FEATS - 1),
            dma(5, FEATS - 1),
            dma(shard_total - 1),
            dma(shard_total - 1),
            dma(ROW_STAGES),
            dma(2),
        ],
        compiler_params=limit(36, 2),
        name="first_layer",
    )(
        slot_cols,
        tile_counts,
        in_hbm(tiles),
        all_feats.reshape(block_total, feat_part, BLK),
        degree_rows,
        back_parts.reshape(SIDE, SIDE, NB, hid_part, BLK),
        own_feats,
        all_weights1,
        bias1.reshape(1, width),
        all_weights2,
        in_hbm(cotangent),
    )

    means, summed = pl.pallas_call(
        last_kernel,
        out_shape=(shape(FEATS, OWN, hid_part, BLK), shape(*pieces, dtype=F32)),
        in_specs=[SMEM, SMEM, HBM, VMEM, VMEM, VMEM],
        out_specs=(VMEM, VMEM),
        scratch_shapes=[
            buf(ROW_STAGES, OWN, *tiles.shape[1:]),
            buf(NB, hid_part, BLK),
            dma(FEATS - 1),
            dma(FEATS - 1),
            dma(shard_total - 1),
            dma(shard_total - 1),
            dma(ROW_STAGES),
        ],
        compiler_params=limit(28, 3),
        name="aggregate_hidden",
    )(
        slot_cols,
        tile_counts,
        in_hbm(tiles),
        all_hidden.reshape(block_total, hid_part, BLK),
        degree_rows,
        piece,
    )
    hidden_out, grad_second, grad_first = pl.pallas_call(
        functools.partial(out_kernel, scale),
        out_shape=(
            shape(own_nodes, width),
            shape(second_rows, width, dtype=F32),
            shape(first_rows, width, dtype=F32),
        ),
        in_specs=[VMEM] * 5,
        out_specs=(VMEM, VMEM, VMEM),
        compiler_params=limit(8),
        name="second_layer",
    )(hidden, means, all_weights2, bias2.reshape(1, width), summed)
    return (
        hidden_out,
        grad_second.reshape(2, hid_part, width),
        grad_first.reshape(2, feat_part, width),
    )


def solution(mesh):
    return jax.shard_map(
        shards,
        mesh=mesh,
        in_specs=(
            P("feat", "node"),
            P("node", None),
            P("node"),
            P("node", None, None, None),
            P("node"),
            P(None, "feat", None),
            P(),
            P(None, "feat", None),
            P(),
            P(("node", "feat"), None),
        ),
        out_specs=(P(("node", "feat"), None), P(None, "feat", None), P(None, "feat", None)),
        check_vma=False,
    )
```

```python
import functools
import math

import jax
import jax.numpy as jnp
from jax import lax
from jax.experimental import pallas as pl
from jax.experimental.pallas import tpu as pltpu
from jax.sharding import PartitionSpec as P

MESH = pl.DeviceIdType.MESH
BF16 = jnp.bfloat16
F32 = jnp.float32
FEATS = 8
SIDE = 4
BLK = 128
NB = 48
OWN = NB // FEATS
HALF, QUARTER = NB // 2, NB // 4
GROUP = 4
BATCH = 8
STAGES = 4
ROW_STAGES = 3
AHEAD = (0, -1, 1, 2)
VMEM = pl.BlockSpec(memory_space=pltpu.VMEM)
SMEM = pl.BlockSpec(memory_space=pltpu.SMEM)
ANY = pl.BlockSpec(memory_space=pl.ANY)
HBM = pl.BlockSpec(memory_space=pltpu.HBM)


def dot(left, right, dims):
    return lax.dot_general(left, right, (dims, ((), ())), preferred_element_type=F32)


class Place:
    def __init__(self):
        self.feat = lax.axis_index("feat")
        self.node = lax.axis_index("node")
        self.x = self.node // SIDE
        self.z = self.node % SIDE

    def peer(self, step):
        return (self.feat + step + FEATS) % FEATS

    def shift(self, dx, dz):
        return ((self.x + dx + SIDE) % SIDE) * SIDE + (self.z + dz + SIDE) % SIDE

    def beside(self):
        return [self.shift(dx, dz) for dx, dz in ((1, 0), (-1, 0), (0, 1), (0, -1))]

    def others(self):
        total = SIDE * SIDE
        return [(self.node + step) % total for step in range(1, total)]

    def turned(self, half, first, second):
        return self.shift(first, second) if half == 0 else self.shift(second, first)

    def greet(self, nodes):
        barrier = pltpu.get_barrier_semaphore()
        others = [{"feat": self.peer(step)} for step in range(1, FEATS)]
        others += [{"node": node} for node in nodes]
        for other in others:
            pl.semaphore_signal(barrier, inc=1, device_id=other, device_id_type=MESH)
        self.greeted = len(others)

    def meet(self):
        pl.semaphore_wait(pltpu.get_barrier_semaphore(), self.greeted)


class Copies:
    def __init__(self):
        self.sent = []

    def send(self, source, target, send_sem, recv_sem, device):
        copy = pltpu.make_async_remote_copy(
            src_ref=source,
            dst_ref=target,
            send_sem=send_sem,
            recv_sem=recv_sem,
            device_id=device,
            device_id_type=MESH,
        )
        copy.start()
        self.sent.append(copy)
        return copy

    def finish(self):
        for copy in self.sent:
            copy.wait_send()


class Regroup:
    def __init__(self, copies, place, source_at, target_at, send_sems, recv_sems):
        self.parts = []
        for step in range(1, FEATS):
            to = place.peer(step)
            self.parts.append(
                copies.send(
                    source_at(to),
                    target_at(place.feat),
                    send_sems.at[step - 1],
                    recv_sems.at[step - 1],
                    {"feat": to},
                )
            )
        target_at(place.feat)[...] = source_at(place.feat)[...]

    def wait(self):
        for part in self.parts:
            part.wait_recv()


class Gather:
    def __init__(self, copies, place, own, out, send_sems, recv_sems):
        self.copies, self.place, self.own, self.out = copies, place, own, out
        self.send_sems, self.recv_sems = send_sems, recv_sems
        self.made = {}

    def _send(self, half, unit, role, source, target, first, second):
        place = self.place
        self.made[half, unit, role] = self.copies.send(
            source,
            target,
            self.send_sems.at[half, unit, role],
            self.recv_sems.at[half, unit, role],
            {"node": place.turned(half, first, second)},
        )

    def full(self, half, unit):
        rows = pl.ds(half * HALF, HALF)
        ahead = 0 if unit == SIDE else AHEAD[unit]
        shard = self.place.turned(half, ahead, 0)
        source = self.own.at[rows] if ahead == 0 else self.out.at[shard, rows]
        for role, way in ((0, 1), (1, -1)):
            move = (way, 0) if unit == SIDE else (0, way)
            self._send(half, unit, role, source, self.out.at[shard, rows], *move)

    def forward(self, half, unit, role):
        way = 1 if role == 0 else -1
        self.made[half, unit, role].wait_recv()
        rows = pl.ds(half * HALF + role * QUARTER, QUARTER)
        if unit == SIDE:
            shard, move = self.place.turned(half, -way, 0), (way, 0)
        else:
            shard, move = self.place.turned(half, AHEAD[unit], -way), (0, way)
        part = self.out.at[shard, rows]
        self._send(half, unit, role + 2, part, part, *move)

    def arrived(self, half, unit):
        for role in (2, 3):
            self.made[half, unit, role].wait_recv()

    def start(self):
        for half in range(2):
            self.full(half, SIDE)

    def start_columns(self):
        for half in range(2):
            self.full(half, 0)

    def rows(self):
        for role in range(2):
            for half in range(2):
                self.forward(half, SIDE, role)
                self.full(half, role + 1)

    def near(self):
        for role in range(2):
            for half in range(2):
                self.forward(half, 0, role)
        for half in range(2):
            self.arrived(half, SIDE)
            self.full(half, 3)

    def far(self, units=(1, 2, 3)):
        for unit in units:
            for role in range(2):
                for half in range(2):
                    self.forward(half, unit, role)

    def last(self):
        for unit in range(SIDE):
            for half in range(2):
                self.arrived(half, unit)


class Scatter:
    def __init__(self, copies, place, parts, bufs, send_sems, recv_sems):
        self.copies, self.place, self.parts = copies, place, parts
        self.pass1, self.got1, self.sum1, self.half1, self.pass2, self.got2, self.sum2 = bufs
        self.send_sems, self.recv_sems = send_sems, recv_sems
        self.made = {}

    def _send(self, half, phase, side, kind, source, target):
        way = 1 if side == 0 else -1
        first, second = (way, 0) if phase == 0 else (0, way)
        self.made[half, phase, side, kind] = self.copies.send(
            source,
            target,
            self.send_sems.at[half, phase, side, kind],
            self.recv_sems.at[half, phase, side, kind],
            {"node": self.place.turned(half, first, second)},
        )

    def _line(self, half, ahead, quarter=None):
        rows = pl.ds(half * HALF, HALF)
        if quarter is not None:
            rows = pl.ds(half * HALF + quarter * QUARTER, QUARTER)
        if half == 0:
            return self.parts.at[(self.place.x + ahead + SIDE) % SIDE, :, rows]
        return self.parts.at[:, (self.place.z + ahead + SIDE) % SIDE, rows]

    def _unit(self, half, ahead, quarter):
        at = self.place.z if half == 0 else self.place.x
        rows = pl.ds(quarter * QUARTER, QUARTER)
        return self.half1.at[half, (at + ahead + SIDE) % SIDE, rows]

    def start(self):
        for half in range(2):
            for side, way in ((0, 1), (1, -1)):
                self._send(half, 0, side, 0, self._line(half, 2 * way, side), self.pass1.at[half, side])

    def direct(self):
        for half in range(2):
            for side, way in ((0, 1), (1, -1)):
                rows = pl.ds((1 - side) * QUARTER, QUARTER)
                self._send(half, 0, side, 1, self._line(half, way, 1 - side), self.got1.at[half, side, :, rows])

    def middle(self):
        for side, way in ((0, 1), (1, -1)):
            for half in range(2):
                self.made[half, 0, side, 0].wait_recv()
                mine, came, total = self._line(half, way, side), self.pass1.at[half, side], self.sum1.at[half, side]

                @pl.loop(0, SIDE)
                def _(shard):
                    total[shard] = (mine[shard].astype(F32) + came[shard].astype(F32)).astype(BF16)

                rows = pl.ds(side * QUARTER, QUARTER)
                self._send(half, 0, side, 2, total, self.got1.at[half, side, :, rows])

    def lines_arrived(self):
        for half in range(2):
            for side in range(2):
                for kind in (1, 2):
                    self.made[half, 0, side, kind].wait_recv()

    def turn(self):
        for half in range(2):
            mine, left, right, total = self._line(half, 0), self.got1.at[half, 0], self.got1.at[half, 1], self.half1.at[half]

            @pl.loop(0, SIDE)
            def _(shard):
                near = left[shard].astype(F32) + right[shard].astype(F32)
                total[shard] = (mine[shard].astype(F32) + near).astype(BF16)

            for side, way in ((0, 1), (1, -1)):
                self._send(half, 1, side, 0, self._unit(half, 2 * way, side), self.pass2.at[half, side])
            for side, way in ((0, 1), (1, -1)):
                rows = pl.ds((1 - side) * QUARTER, QUARTER)
                self._send(half, 1, side, 1, self._unit(half, way, 1 - side), self.got2.at[half, side, rows])

    def middle2(self):
        for side, way in ((0, 1), (1, -1)):
            for half in range(2):
                self.made[half, 1, side, 0].wait_recv()
                total = self.sum2.at[half, side]
                mine, came = self._unit(half, way, side)[...], self.pass2[half, side]
                total[...] = (mine.astype(F32) + came.astype(F32)).astype(BF16)
                rows = pl.ds(side * QUARTER, QUARTER)
                self._send(half, 1, side, 2, total, self.got2.at[half, side, rows])

    def end(self, out):
        for half in range(2):
            for side in range(2):
                for kind in (1, 2):
                    self.made[half, 1, side, kind].wait_recv()
            for quarter in range(2):
                rows = pl.ds(quarter * QUARTER, QUARTER)
                near = self.got2[half, 0, rows].astype(F32) + self.got2[half, 1, rows].astype(F32)
                total = self._unit(half, 0, quarter)[...].astype(F32) + near
                out[pl.ds(half * HALF + quarter * QUARTER, QUARTER)] = total.astype(BF16)


class Rows:
    def __init__(self, place, cols, counts, tiles, source, degrees, mean, means, held, send_sems, recv_sems, tile_sems):
        self.place, self.cols, self.counts, self.tiles, self.source = place, cols, counts, tiles, source
        self.degrees, self.mean, self.means, self.held = degrees, mean, means, held
        self.send_sems, self.recv_sems, self.tile_sems = send_sems, recv_sems, tile_sems
        for step in range(ROW_STAGES - 1):
            self.fetch(step).start()

    def fetch(self, step):
        slot = step % ROW_STAGES
        rows = own_rows(self.place.peer(step + 1))
        return pltpu.make_async_copy(self.tiles.at[rows], self.held.at[slot], self.tile_sems.at[slot])

    def give(self, step):
        to = self.place.peer(step + 1)
        return pltpu.make_async_remote_copy(
            src_ref=self.mean.at[own_rows(to)],
            dst_ref=self.means.at[self.place.feat],
            send_sem=self.send_sems.at[step],
            recv_sem=self.recv_sems.at[step],
            device_id={"feat": to},
            device_id_type=MESH,
        )

    def work(self, step):
        self.fetch(step).wait()
        slots = self.tiles.shape[1]
        for part in range(OWN):
            block = self.place.peer(step + 1) * OWN + part
            parts = []
            for slot in range(slots):
                value = self.source[self.cols[slot, block]]
                parts.append(jnp.where(slot < self.counts[block], value, jnp.zeros_like(value)))
            wide = jnp.concatenate([self.held[step % ROW_STAGES, part, slot] for slot in range(slots)], axis=1)
            total = dot(jnp.concatenate(parts, axis=1), wide, ((1,), (1,)))
            self.mean[block] = (total / self.degrees[pl.ds(block, 1), :].astype(F32)).astype(BF16)

    def first(self):
        self.fetch(ROW_STAGES - 1).start()
        self.work(0)

    def run(self, first, last):
        def body(step, carry):
            @pl.when(step + ROW_STAGES - 1 < FEATS)
            def _():
                self.fetch(step + ROW_STAGES - 1).start()

            self.work(step)
            self.give(step).start()
            return carry

        lax.fori_loop(first, last, body, jnp.int32(0))

    def own(self):
        self.work(FEATS - 1)
        self.means[self.place.feat] = self.mean[own_rows(self.place.feat)]

    def wait(self):
        for step in range(FEATS - 1):
            self.give(step).wait()


class Exchange:
    def __init__(self, copies, place, source_at, target, send_sems, recv_sems):
        self.parts = []
        for number, node in enumerate(place.others()):
            self.parts.append(
                copies.send(
                    source_at(node), target.at[place.node], send_sems.at[number], recv_sems.at[number], {"node": node}
                )
            )

    def wait(self):
        for part in self.parts:
            part.wait_recv()


def own_rows(feat):
    return pl.ds(feat * OWN, OWN)


def gather_kernel(
    features_in, weights1, weights2, cotangent_in, degrees_in,
    all_feats, own_feats, all_weights1, all_weights2, spread,
    features, cotangent, degrees, own_weights1, own_weights2, blocks, outgoing,
    gather_send, gather_recv, feat_send, feat_recv, local_sems,
):
    place, copies = Place(), Copies()
    pairs = (
        (features_in, features),
        (weights2, own_weights2),
        (weights1, own_weights1),
        (cotangent_in, cotangent),
        (degrees_in, degrees),
    )
    loads = [pltpu.make_async_copy(pair[0], pair[1], local_sems.at[number]) for number, pair in enumerate(pairs)]
    for load in loads:
        load.start()
    place.greet(place.beside())
    loads[0].wait()
    for block in range(NB):
        blocks[block] = features[:, block * BLK : (block + 1) * BLK]
    place.meet()
    gather = Gather(copies, place, blocks, all_feats, gather_send, gather_recv)
    gather.start()
    gather.start_columns()
    loads[3].wait()
    loads[4].wait()
    for block in range(OWN):
        nodes = jnp.transpose(cotangent[block * BLK : (block + 1) * BLK, :].astype(F32))
        degree = degrees[pl.ds(place.feat * OWN + block, 1), :].astype(F32)
        outgoing[:, block] = (nodes / degree).astype(BF16).reshape(FEATS, -1, BLK)
    regroups = [
        Regroup(
            copies, place, lambda to: outgoing.at[to], lambda slot: spread.at[slot], feat_send.at[3], feat_recv.at[3]
        )
    ]
    for number, (weights, target) in enumerate(((own_weights2, all_weights2), (own_weights1, all_weights1))):
        loads[1 + number].wait()
        regroups.append(
            Regroup(
                copies, place, lambda to: weights, lambda slot: target.at[slot], feat_send.at[number], feat_recv.at[number]
            )
        )
    own = pltpu.make_async_copy(blocks, all_feats.at[place.node], local_sems.at[len(pairs)])
    own.start()
    gather.rows()
    gather.near()
    regroups.append(
        Regroup(
            copies, place, lambda to: blocks.at[own_rows(to)], lambda slot: own_feats.at[slot], feat_send.at[2], feat_recv.at[2]
        )
    )
    gather.far()
    for regroup in regroups:
        regroup.wait()
    gather.last()
    own.wait()
    copies.finish()


def plan_groups(counts, groups):
    def row(block, total):
        for part in range(4):
            groups[total + part] = block * 4 + part
        return total + (counts[block] + GROUP - 1) // GROUP

    total = lax.fori_loop(0, NB, row, jnp.int32(0))
    for part in range(BATCH):
        groups[total + part] = 0
    return total


def each_step(counts, groups, tiles, held, tile_sems, clear, work):
    total = plan_groups(counts, groups)
    steps = (total + BATCH - 1) // BATCH

    def fetch(step):
        @pl.when(step < steps)
        def _():
            slot = step % STAGES
            for place in range(BATCH):
                group = groups[step * BATCH + place]
                pltpu.make_async_copy(tiles.at[group], held.at[slot, place], tile_sems.at[slot]).start()

    for step in range(STAGES - 1):
        fetch(step)
    clear()

    def body(step, carry):
        fetch(step + STAGES - 1)
        slot = step % STAGES
        pltpu.make_async_copy(tiles.at[pl.ds(0, BATCH)], held.at[slot], tile_sems.at[slot]).wait()
        entries = []
        for place in range(BATCH):
            group = groups[step * BATCH + place]
            block, first = group // 4, (group % 4) * GROUP
            live = jnp.where(step * BATCH + place < total, counts[block], 0)
            wide = jnp.concatenate([held[slot, place, part] for part in range(GROUP)], axis=1)
            entries.append((block, first, live, wide))
        work(entries)
        return carry

    lax.fori_loop(0, steps, body, jnp.int32(0))


def load_all(pairs, sems):
    loads = [pltpu.make_async_copy(pair[0], pair[1], sems.at[number]) for number, pair in enumerate(pairs)]
    for load in loads:
        load.start()
    for load in loads:
        load.wait()


def back_kernel(cols_in, counts_in, tiles, spread, back, cols, counts, held, sums, groups, tile_sems, load_sems):
    load_all(((cols_in, cols), (counts_in, counts)), load_sems)

    def clear():
        @pl.loop(0, sums.shape[0] // 16)
        def _(part):
            sums[pl.ds(part * 16, 16)] = jnp.zeros((16,) + sums.shape[1:], F32)

    def work(entries):
        backs = [dot(spread[entry[0]], entry[3], ((1,), (0,))) for entry in entries]
        for (block, first, live, _), product in zip(entries, backs):
            for slot in range(GROUP):
                part = product[:, slot * BLK : (slot + 1) * BLK]
                sums[cols[first + slot, block]] += jnp.where(first + slot < live, part, jnp.zeros_like(part))

    each_step(counts, groups, tiles, held, tile_sems, clear, work)

    @pl.loop(0, sums.shape[0] // 16)
    def _(part):
        rows = pl.ds(part * 16, 16)
        back[rows] = sums[rows].astype(BF16)


def put_tiles(out, kind, first, value):
    for tile in range(value.shape[0] // 4):
        out[first + tile, kind] = value[tile // 2 * 8 : tile // 2 * 8 + 8, tile % 2 * BLK : tile % 2 * BLK + BLK]


def middle_kernel(
    cols, counts, tiles, all_feats, degrees, back_parts, own_feats, weights1, bias1, weights2, cotangent_in,
    all_hidden, hidden, piece,
    held, cotangent, feat_mean, means, slopes, selves, own_hidden, back, own_back,
    grads, feat_buf, early, early_buf, part, came, bufs,
    gather_send, gather_recv, scatter_send, scatter_recv, feat_send, feat_recv, total_send, total_recv,
    tile_sems, local_sems,
):
    place, copies = Place(), Copies()

    rows = Rows(
        place, cols, counts, tiles, all_feats, degrees, feat_mean, means, held, feat_send.at[0], feat_recv.at[0], tile_sems
    )
    load = pltpu.make_async_copy(cotangent_in, cotangent, local_sems.at[0])
    load.start()
    place.greet(place.others())
    place.meet()

    def regroup(number, source_at, target_at):
        return Regroup(copies, place, source_at, target_at, feat_send.at[number], feat_recv.at[number])

    scatter = Scatter(copies, place, back_parts, bufs, scatter_send, scatter_recv)
    scatter.start()
    first = weights1[...].reshape(-1, weights1.shape[-1])
    bias = jnp.transpose(jnp.broadcast_to(bias1[...], (BLK, bias1.shape[1])))
    rows.run(0, 3)
    scatter.direct()
    rows.run(3, FEATS - 1)
    rows.own()
    scatter.middle()
    rows.wait()

    def stack(block):
        parts = []
        for part in range(FEATS):
            parts += [own_feats[part, block], means[part, block]]
        return jnp.concatenate(parts, axis=0)

    for block in range(OWN):
        pre = dot(first, stack(block), ((0,), (0,))) + bias
        sigmoid = jax.nn.sigmoid(pre)
        slopes[:, block * BLK : (block + 1) * BLK] = (sigmoid * (1.0 + pre * (1.0 - sigmoid))).astype(BF16)
        hidden[:, block] = (pre * sigmoid).astype(BF16).reshape(FEATS, -1, BLK)
    to_hidden = regroup(1, lambda to: hidden.at[to], lambda slot: own_hidden.at[own_rows(slot)])
    own_weights = weights2[:, 0].reshape(-1, weights2.shape[-1])
    load.wait()
    selves[...] = dot(own_weights, cotangent[...], ((1,), (1,)))
    all_blocks = jnp.concatenate([hidden[:, block].reshape(-1, BLK) for block in range(OWN)], axis=1)
    total = dot(all_blocks, cotangent[...], ((1,), (0,)))
    early[...] = total.reshape(early.shape)
    to_hidden.wait()
    to_early = regroup(4, lambda to: early.at[to], lambda slot: early_buf.at[slot])
    gather = Gather(copies, place, own_hidden, all_hidden, gather_send, gather_recv)
    own = pltpu.make_async_copy(own_hidden, all_hidden.at[place.node], local_sems.at[1])
    own.start()
    scatter.lines_arrived()
    gather.start()
    scatter.turn()
    scatter.middle2()
    gather.start_columns()
    gather.rows()
    scatter.end(back)
    to_back = regroup(2, lambda to: back.at[own_rows(to)], lambda slot: own_back.at[slot])
    neighbour = weights2[:, 1].reshape(-1, weights2.shape[-1])
    first_stack = jnp.concatenate([stack(block) for block in range(OWN)], axis=1)
    to_back.wait()
    came_back = jnp.concatenate(
        [own_back[:, block].reshape(-1, BLK) for block in range(OWN)], axis=1
    )
    grad = selves[...] + dot(neighbour, came_back, ((1,), (0,)))
    grad = (grad * slopes[...].astype(F32)).astype(BF16)
    first_rows, hid_rows = weights1.shape[1] * weights1.shape[2], weights2.shape[2]
    grads[:, :first_rows] = dot(first_stack, grad, ((1,), (1,))).reshape(FEATS, first_rows, -1)
    all_blocks = jnp.concatenate([hidden[:, block].reshape(-1, BLK) for block in range(OWN)], axis=1)
    grads[:, first_rows:] = dot(all_blocks, came_back, ((1,), (1,))).reshape(FEATS, hid_rows, -1)
    to_total = regroup(3, lambda to: grads.at[to], lambda slot: feat_buf.at[slot])
    part[...] = jnp.zeros_like(part)
    to_early.wait()
    put_tiles(part, 0, 0, sum(early_buf[slot] for slot in range(FEATS)))
    gather.near()
    gather.far((1, 2))
    to_total.wait()
    summed = sum(feat_buf[slot] for slot in range(FEATS))
    put_tiles(part, 0, hid_rows // 4, summed[first_rows:])
    put_tiles(part, 1, 0, summed[:first_rows])
    exchange = Exchange(copies, place, lambda node: part.at[node], came, total_send, total_recv)
    came[place.node] = part[place.node]
    gather.far((3,))
    gather.last()
    exchange.wait()
    piece[...] = sum(came[slot] for slot in range(SIDE * SIDE))
    own.wait()
    copies.finish()


def last_kernel(
    cols, counts, tiles, all_hidden, degrees, piece,
    means, summed,
    held, hidden_mean, feat_send, feat_recv, total_send, total_recv, tile_sems,
):
    place, copies = Place(), Copies()
    rows = Rows(
        place, cols, counts, tiles, all_hidden, degrees, hidden_mean, means, held, feat_send, feat_recv, tile_sems
    )
    place.greet(place.others())
    rows.first()
    place.meet()
    rows.give(0).start()
    exchange = Exchange(copies, place, lambda node: piece, summed, total_send, total_recv)
    summed[place.node] = piece[...]
    rows.run(1, FEATS - 1)
    rows.own()
    rows.wait()
    exchange.wait()
    copies.finish()


def out_kernel(scale, hidden, means, weights2, bias2, summed, hidden_out, grad_second, grad_first):
    second = weights2[...].reshape(-1, weights2.shape[-1])
    for block in range(OWN):
        parts = []
        for part in range(FEATS):
            parts += [hidden[part, block], means[part, block]]
        out = dot(jnp.concatenate(parts, axis=0), second, ((0,), (0,))) + bias2[...]
        hidden_out[block * BLK : (block + 1) * BLK, :] = out.astype(BF16)
    for kind, grad in enumerate((grad_second, grad_first)):
        for tile in range(grad.shape[0] // 8 * 2):
            rows, columns = pl.ds(tile // 2 * 8, 8), pl.ds(tile % 2 * BLK, BLK)
            grad[rows, columns] = summed[tile, kind] * scale


def limit(mib, collective_id=None):
    if collective_id is None:
        return pltpu.CompilerParams(vmem_limit_bytes=mib * 1024 * 1024)
    return pltpu.CompilerParams(
        collective_id=collective_id, has_side_effects=True, vmem_limit_bytes=mib * 1024 * 1024
    )


def shape(*dims, dtype=BF16):
    return jax.ShapeDtypeStruct(dims, dtype)


def buf(*dims, dtype=BF16):
    return pltpu.VMEM(dims, dtype)


def dma(*dims):
    return pltpu.SemaphoreType.DMA(dims)


def in_hbm(array):
    return pltpu.with_memory_space_constraint(array, pltpu.HBM)


def shards(
    features, tile_cols, tile_counts, tiles, degrees, weights1, bias1, weights2, bias2, cotangent
):
    feat_part = features.shape[0]
    hid_part = weights2.shape[1]
    width = weights2.shape[2]
    shard_total = lax.axis_size("node")
    block_total = shard_total * NB
    scale = 1.0 / math.sqrt(features.shape[1] * shard_total)
    own_nodes = OWN * BLK
    degree_rows = degrees.reshape(NB, BLK)
    groups = tiles.reshape(NB * tiles.shape[1] // GROUP, GROUP, BLK, BLK)

    all_feats, own_feats, all_weights1, all_weights2, spread = pl.pallas_call(
        gather_kernel,
        out_shape=(
            shape(shard_total, NB, feat_part, BLK),
            shape(FEATS, OWN, feat_part, BLK),
            shape(FEATS, 2, feat_part, width),
            shape(FEATS, 2, hid_part, width),
            shape(FEATS, OWN, hid_part, BLK),
        ),
        in_specs=[HBM] * 5,
        out_specs=(ANY, VMEM, VMEM, VMEM, VMEM),
        scratch_shapes=[
            buf(*features.shape),
            buf(own_nodes, width),
            buf(NB, BLK, dtype=jnp.int32),
            buf(*weights1.shape),
            buf(*weights2.shape),
            buf(NB, feat_part, BLK),
            buf(FEATS, OWN, hid_part, BLK),
            dma(2, 5, 4),
            dma(2, 5, 4),
            dma(4, FEATS - 1),
            dma(4, FEATS - 1),
            dma(6),
        ],
        compiler_params=limit(12, 1),
        name="gather_features",
    )(*[in_hbm(array) for array in (features, weights1, weights2, cotangent, degree_rows)])

    held = buf(STAGES, BATCH, GROUP, BLK, BLK)
    planned = pltpu.SMEM((NB * 4 + 2 * BATCH,), jnp.int32)
    slot_cols = tile_cols.T
    listed = [pltpu.SMEM((tiles.shape[1], NB), jnp.int32), pltpu.SMEM((NB,), jnp.int32)]
    back_parts = pl.pallas_call(
        back_kernel,
        out_shape=shape(block_total, hid_part, BLK),
        in_specs=[HBM, HBM, HBM, VMEM],
        out_specs=VMEM,
        scratch_shapes=[
            *listed,
            held,
            buf(block_total, hid_part, BLK, dtype=F32),
            planned,
            dma(STAGES),
            dma(2),
        ],
        compiler_params=limit(28),
        name="aggregate_back",
    )(in_hbm(slot_cols), in_hbm(tile_counts), in_hbm(groups), spread.reshape(NB, hid_part, BLK))

    row = (SIDE, HALF, hid_part, BLK)
    part_row = (SIDE, QUARTER, hid_part, BLK)
    middle_bufs = (
        buf(2, 2, *part_row),
        buf(2, 2, *row),
        buf(2, 2, *part_row),
        buf(2, *row),
        buf(2, 2, *part_row[1:]),
        buf(2, 2, *row[1:]),
        buf(2, 2, *part_row[1:]),
    )
    first_rows, second_rows = 2 * feat_part, 2 * hid_part
    pieces = (shard_total, 2, 8, BLK)
    all_hidden, hidden, piece = pl.pallas_call(
        middle_kernel,
        out_shape=(
            shape(shard_total, NB, hid_part, BLK),
            shape(FEATS, OWN, hid_part, BLK),
            shape(*pieces[1:], dtype=F32),
        ),
        in_specs=[SMEM, SMEM, HBM] + [VMEM] * 7 + [HBM],
        out_specs=(ANY, VMEM, VMEM),
        scratch_shapes=[
            buf(ROW_STAGES, OWN, *tiles.shape[1:]),
            buf(own_nodes, width),
            buf(NB, feat_part, BLK),
            buf(FEATS, OWN, feat_part, BLK),
            buf(width, own_nodes),
            buf(width, own_nodes, dtype=F32),
            buf(NB, hid_part, BLK),
            buf(NB, hid_part, BLK),
            buf(FEATS, OWN, hid_part, BLK),
            buf(FEATS, first_rows + hid_part, width, dtype=F32),
            buf(FEATS, first_rows + hid_part, width, dtype=F32),
            buf(FEATS, hid_part, width, dtype=F32),
            buf(FEATS, hid_part, width, dtype=F32),
            buf(*pieces, dtype=F32),
            buf(*pieces, dtype=F32),
            middle_bufs,
            dma(2, 5, 4),
            dma(2, 5, 4),
            dma(2, 2, 2, 3),
            dma(2, 2, 2, 3),
            dma(5, FEATS - 1),
            dma(5, FEATS - 1),
            dma(shard_total - 1),
            dma(shard_total - 1),
            dma(ROW_STAGES),
            dma(2),
        ],
        compiler_params=limit(36, 2),
        name="first_layer",
    )(
        slot_cols,
        tile_counts,
        in_hbm(tiles),
        all_feats.reshape(block_total, feat_part, BLK),
        degree_rows,
        back_parts.reshape(SIDE, SIDE, NB, hid_part, BLK),
        own_feats,
        all_weights1,
        bias1.reshape(1, width),
        all_weights2,
        in_hbm(cotangent),
    )

    means, summed = pl.pallas_call(
        last_kernel,
        out_shape=(shape(FEATS, OWN, hid_part, BLK), shape(*pieces, dtype=F32)),
        in_specs=[SMEM, SMEM, HBM, VMEM, VMEM, VMEM],
        out_specs=(VMEM, VMEM),
        scratch_shapes=[
            buf(ROW_STAGES, OWN, *tiles.shape[1:]),
            buf(NB, hid_part, BLK),
            dma(FEATS - 1),
            dma(FEATS - 1),
            dma(shard_total - 1),
            dma(shard_total - 1),
            dma(ROW_STAGES),
        ],
        compiler_params=limit(28, 3),
        name="aggregate_hidden",
    )(
        slot_cols,
        tile_counts,
        in_hbm(tiles),
        all_hidden.reshape(block_total, hid_part, BLK),
        degree_rows,
        piece,
    )
    hidden_out, grad_second, grad_first = pl.pallas_call(
        functools.partial(out_kernel, scale),
        out_shape=(
            shape(own_nodes, width),
            shape(second_rows, width, dtype=F32),
            shape(first_rows, width, dtype=F32),
        ),
        in_specs=[VMEM] * 5,
        out_specs=(VMEM, VMEM, VMEM),
        compiler_params=limit(8),
        name="second_layer",
    )(hidden, means, all_weights2, bias2.reshape(1, width), summed)
    return (
        hidden_out,
        grad_second.reshape(2, hid_part, width),
        grad_first.reshape(2, feat_part, width),
    )


def solution(mesh):
    return jax.shard_map(
        shards,
        mesh=mesh,
        in_specs=(
            P("feat", "node"),
            P("node", None),
            P("node"),
            P("node", None, None, None),
            P("node"),
            P(None, "feat", None),
            P(),
            P(None, "feat", None),
            P(),
            P(("node", "feat"), None),
        ),
        out_specs=(P(("node", "feat"), None), P(None, "feat", None), P(None, "feat", None)),
        check_vma=False,
    )
```
